256 devices in a mesh: ctx: 32 (over x, y, core), exp: 8 (over z).
Axes of the slice: x: 4, y: 4, z: 8, core: 2. Of those that a mesh axis runs over, the one named last changes fastest.
Arguments:
- residual: bfloat16 [2, 2048, 4096], P(None, 'ctx', 'exp'), may hold values from -3 to 3
- queries: bfloat16 [2, 2048, 4096], P(None, 'ctx', 'exp'), may hold values from -40 to 40
- cache_kv: bfloat16 [2, 2, 6144, 1024], P(None, None, 'ctx', 'exp'), may hold values from -4 to 4
- fresh_key_value: bfloat16 [2, 2, 2048, 1024], P(None, None, 'ctx', 'exp'), may hold values from -6 to 6
- out_weight: bfloat16 [4096, 4096], P('exp'), may hold values from -1 to 1
- norm_gain: float32 [4096], replicated, may hold values from 0.3 to 3
- router_weight: bfloat16 [4096, 8], replicated, may hold values from -0.09375 to 0.09375
- gate_weight: bfloat16 [8, 4096, 10240], P('exp', None, 'ctx'), may hold values from -0.09375 to 0.09375
- up_weight: bfloat16 [8, 4096, 10240], P('exp', None, 'ctx'), may hold values from -0.09375 to 0.09375
- down_weight: bfloat16 [8, 10240, 4096], P('exp', 'ctx'), may hold values from -0.125 to 0.125
- expert_ids: int32 [2048, 2, 2], P('ctx'), may hold values from 0 to 7, all different within a row; in each aligned block of 128 rows (0 to 127, 128 to 255, ..., all dimensions but the last counted through in order) at most 32 rows name the same one
Outputs:
- layer_out: bfloat16 [2, 2048, 4096], P(None, 'ctx', 'exp')
The draws below stay inside these ranges and needn't reach their ends.
Inputs may be any that keep to these rules, and one draw needn't show every extreme that they name: `expert_ids`: A token's two experts differ. Within each device's aligned block of 128 rows (its 64 positions of both traces), every expert is named exactly 32 times.
All inputs are finite; a program needn't handle non-finite values.
Results may differ from the reference program's by a relative error of at most 0.023.
Values may be sent and summed in bfloat16 or wider, within the bound.
No kernel may reach another device: no remote copies, remote signals or barrier semaphores. Data moves between devices by JAX's collectives and lax.ppermute only.
A program may use at most 128 MiB of HBM per device.

```python
import math
import jax
import jax.numpy as jnp
import numpy as np
from jax import lax

D = 4096
HEAD_WIDTH = 128
HEADS_PER_GROUP = 4
KEY_VALUE_HEADS = 8
QUERY_HEADS = 32
EXPERTS = 8
TOP = 2
FF = 10240
PACKET_TRACES = 2
NEW_POSITIONS = 2048
CACHED_POSITIONS = 6144
TOK_DEV = 128
TOKENS = 4096
CAP_DEV = 32
N_CTX = 32


def pair_draw(key):
    query_key, cached_keys = jax.random.split(jax.random.fold_in(key, 11))
    query_values = 2.0 * jnp.clip(jax.random.normal(query_key, (PACKET_TRACES, NEW_POSITIONS, QUERY_HEADS * HEAD_WIDTH), jnp.float32), -4.0, 4.0)
    cached_values = jnp.clip(jax.random.normal(cached_keys, (2, PACKET_TRACES, CACHED_POSITIONS, KEY_VALUE_HEADS * HEAD_WIDTH), jnp.float32), -4.0, 4.0)
    return (query_values, cached_values)


def draw_queries(key, part):
    return pair_draw(key)[0].astype(jnp.bfloat16)


def draw_cache_kv(key, part):
    return pair_draw(key)[1].astype(jnp.bfloat16)


def block_levels(stream_key, extent, cuts, smallest, top_value):
    level, own = 1.0, jax.random.fold_in(stream_key, 6)
    for dim, parts in cuts:
        draws = jnp.exp(jax.random.uniform(jax.random.fold_in(own, dim), (parts,), jnp.float32, smallest / len(cuts), top_value / len(cuts)))
        level = level * jnp.repeat(draws, extent[dim] // parts).reshape([-1 if axis == dim else 1 for axis in range(len(extent))])
    return level


def deal_out(key, own, number, rows, amount, top, bound, slope):
    order = jax.random.permutation(key, amount)
    crowded, common = shares(amount, rows * top, bound, slope, True), shares(amount, rows * top, bound, slope, False)
    places = jnp.arange(amount)

    def named(lengths, offset_by):
        used = int((lengths > 0).sum())
        fixed = max(1, used // 4)
        passed = fixed + (places - fixed + offset_by * (used - fixed)) % max(1, amount - fixed)
        return jnp.zeros((amount,), jnp.int32).at[order[jnp.where(places < fixed, places, passed)]].set(jnp.asarray(lengths, jnp.int32))

    lengths = jnp.where(number % 4 == 0, named(crowded, number // 4), named(common, number - number // 4 - 1))
    mixed = jax.random.permutation(jax.random.fold_in(own, 3), amount)
    source_of, receiver = mixed[0:amount // 2 * 2:2], mixed[1:amount // 2 * 2:2]
    slack = jnp.minimum(lengths[source_of] - 1, bound - lengths[receiver]) // 2
    slack = jnp.where((source_of == order[0]) | (receiver == order[0]) | (lengths[receiver] == 0), 0, jnp.maximum(slack, 0))
    passed = jax.random.randint(jax.random.fold_in(own, 4), (amount // 2,), 0, 1 << 20) % (slack + 1)
    lengths = lengths.at[source_of].add(-passed).at[receiver].add(passed)
    items = jnp.searchsorted(jnp.cumsum(lengths), jnp.arange(rows * top), side="right").astype(jnp.int32)
    table = items.reshape(top, rows).T
    table = table[jax.random.permutation(jax.random.fold_in(own, 1), rows)]
    offset_by = jax.random.randint(jax.random.fold_in(own, 2), (rows, 1), 0, top)
    return jnp.take_along_axis(table, (jnp.arange(top)[None, :] + offset_by) % top, axis=1)


def shares(number_of, total, bound, lean, full):
    weights = [(1 << 20) // math.isqrt(grade ** lean) + 1 for grade in range(1, number_of + 1)]
    largest = bound if full else min(bound, max(-(-total // number_of), total * weights[0] // sum(weights)))
    least = 1 if total - largest >= number_of - 1 else 0
    holding, spare = [largest] + [least] * (number_of - 1), total - largest - least * (number_of - 1)
    while spare > 0:
        candidates = [i for i in range(1, number_of) if holding[i] < largest] or [i for i in range(1, number_of) if holding[i] < bound]
        pool, remaining = sum([weights[i] for i in candidates]), spare
        for i in candidates:
            addition = min(bound - holding[i], max(1, remaining * weights[i] // pool), spare)
            holding[i] = holding[i] + addition
            spare = spare - addition
    return np.array(holding)


def scatter_about(stream_key, extent, deviation, bound, shards=(), held_as=jnp.bfloat16):
    factor_of = block_levels(stream_key, extent, shards, -0.22, 0.18) if shards else 1.0
    entries = jax.random.normal(stream_key, extent, jnp.float32) * deviation * factor_of
    return jnp.minimum(jnp.maximum(entries, -bound), bound).astype(held_as)


def setup_inputs(seed: int = 0) -> dict:
    splits = jax.random.split(jax.random.key(seed), 12)
    residual = scatter_about(splits[0], (PACKET_TRACES, NEW_POSITIONS, D), 0.5, 3.0, ((1, 32), (2, 8)))
    queries = draw_queries(jax.random.fold_in(splits[11], 71), 0)
    cache_kv = draw_cache_kv(jax.random.fold_in(splits[11], 71), 0)
    fresh_key_value = scatter_about(splits[3], (2, PACKET_TRACES, NEW_POSITIONS, KEY_VALUE_HEADS * HEAD_WIDTH), 1.0, 6.0, ((2, 32), (3, 8)))
    out_weight = scatter_about(splits[4], (QUERY_HEADS * HEAD_WIDTH, D), (HEAD_WIDTH // 4) ** -0.5, 1.0, ((0, 8),))
    norm_gain = jnp.clip(jnp.exp(jax.random.uniform(splits[5], (D,), jnp.float32, math.log(0.3), math.log(3.0))), 0.3, 3.0)
    router_weight = scatter_about(splits[6], (D, EXPERTS), D ** -0.5, 0.09375)
    gate_weight = scatter_about(splits[7], (EXPERTS, D, FF), D ** -0.5, 0.09375, ((0, 8), (2, 32)))
    up_weight = scatter_about(splits[8], (EXPERTS, D, FF), D ** -0.5, 0.09375, ((0, 8), (2, 32)))
    down_weight = scatter_about(splits[9], (EXPERTS, FF, D), (FF // 4) ** -0.5, 0.125, ((0, 8), (1, 32)))
    expert_ids_keys = jax.random.split(jax.random.fold_in(splits[10], 1), NEW_POSITIONS * PACKET_TRACES // TOK_DEV)
    expert_ids_turns = jax.random.permutation(jax.random.fold_in(splits[10], 3), NEW_POSITIONS * PACKET_TRACES // TOK_DEV)
    expert_ids = jax.vmap(lambda own, number: deal_out(jax.random.fold_in(splits[10], 2), own, number, TOK_DEV, EXPERTS, TOP, CAP_DEV, 0))(expert_ids_keys, expert_ids_turns).reshape((NEW_POSITIONS, PACKET_TRACES, TOP))
    return dict(residual=residual, queries=queries, cache_kv=cache_kv, fresh_key_value=fresh_key_value, out_weight=out_weight, norm_gain=norm_gain, router_weight=router_weight, gate_weight=gate_weight, up_weight=up_weight, down_weight=down_weight, expert_ids=expert_ids)


def reference(residual, queries, cache_kv, fresh_key_value, out_weight, norm_gain, router_weight, gate_weight, up_weight, down_weight, expert_ids):
    score_scale = 1.0 / math.sqrt(HEAD_WIDTH)
    positions = jnp.arange(CACHED_POSITIONS + NEW_POSITIONS, dtype=jnp.int32)
    query_pos = jnp.arange(NEW_POSITIONS, dtype=jnp.int32)
    visible = positions[None, :] - CACHED_POSITIONS <= query_pos[:, None]
    head_parts = []
    for trace_index in range(PACKET_TRACES):
        keys_all = jnp.concatenate((cache_kv[0, trace_index], fresh_key_value[0, trace_index]), axis=0)
        values_all = jnp.concatenate((cache_kv[1, trace_index], fresh_key_value[1, trace_index]), axis=0)
        query_trace = queries[trace_index]

        def single_group(group_index):
            query_block = lax.dynamic_slice_in_dim(query_trace, group_index * HEADS_PER_GROUP * HEAD_WIDTH, HEADS_PER_GROUP * HEAD_WIDTH, 1)
            query_block = query_block.reshape(NEW_POSITIONS, HEADS_PER_GROUP, HEAD_WIDTH).astype(jnp.float32)
            key_block = lax.dynamic_slice_in_dim(keys_all, group_index * HEAD_WIDTH, HEAD_WIDTH, 1).astype(jnp.float32)
            value_block = lax.dynamic_slice_in_dim(values_all, group_index * HEAD_WIDTH, HEAD_WIDTH, 1).astype(jnp.float32)
            scores = jnp.einsum('jgd,rd->gjr', query_block, key_block) * score_scale
            scores = jnp.where(visible[None], scores, -1e+30)
            highest = lax.optimization_barrier(jnp.max(scores, axis=2, keepdims=True))
            weights = jnp.where(visible[None], jnp.exp(scores - highest), 0.0)
            totals = lax.optimization_barrier(jnp.sum(weights, axis=2))
            probability = lax.optimization_barrier(weights.astype(jnp.bfloat16)).astype(jnp.float32)
            mixture = jnp.einsum('gjr,rd->jgd', probability, value_block) / jnp.transpose(totals)[:, :, None]
            return mixture.astype(jnp.bfloat16)
        grouped_queries = lax.map(single_group, jnp.arange(KEY_VALUE_HEADS, dtype=jnp.int32))
        head_parts.append(jnp.transpose(grouped_queries, (1, 0, 2, 3)).reshape(NEW_POSITIONS, QUERY_HEADS * HEAD_WIDTH))
    head_rows = jnp.concatenate(head_parts, axis=0)
    hidden_state = residual.reshape(TOKENS, D).astype(jnp.float32) + jnp.dot(head_rows, out_weight, preferred_element_type=jnp.float32)
    normed = (hidden_state * lax.rsqrt(lax.optimization_barrier(jnp.mean(hidden_state * hidden_state, axis=1, keepdims=True)) + 1e-05) * norm_gain).astype(jnp.bfloat16)
    logits = jnp.dot(normed, router_weight, preferred_element_type=jnp.float32)
    picked = jnp.transpose(expert_ids, (1, 0, 2)).reshape(TOKENS, TOP)
    picked_logits = jnp.take_along_axis(logits, picked, axis=1)
    gate_values = jax.nn.sigmoid(picked_logits - picked_logits[:, ::-1])
    per_expert = TOKENS * TOP // EXPERTS
    slice_width = FF // N_CTX
    combined = jnp.zeros((TOKENS, D), jnp.float32)
    for expert in range(EXPERTS):
        matches = picked == expert
        row_index = jnp.nonzero(jnp.any(matches, axis=1), size=per_expert)[0].astype(jnp.int32)
        inputs = normed[row_index]
        gate_part = jnp.dot(inputs, gate_weight[expert], preferred_element_type=jnp.float32)
        up_part = jnp.dot(inputs, up_weight[expert], preferred_element_type=jnp.float32)
        activated = (jax.nn.silu(gate_part) * up_part).astype(jnp.bfloat16)
        down_expert = down_weight[expert]

        def add_slice(running, slice_index):
            hidden_piece = lax.dynamic_slice_in_dim(activated, slice_index * slice_width, slice_width, 1)
            weight_piece = lax.dynamic_slice_in_dim(down_expert, slice_index * slice_width, slice_width, 0)
            partial_value = jnp.dot(hidden_piece, weight_piece, preferred_element_type=jnp.float32).astype(jnp.bfloat16)
            partial_value = lax.optimization_barrier(partial_value)
            return (running + partial_value.astype(jnp.float32), None)
        summed, _ = lax.scan(add_slice, jnp.zeros((per_expert, D), jnp.float32), jnp.arange(N_CTX, dtype=jnp.int32))
        expert_out = lax.optimization_barrier(summed.astype(jnp.bfloat16)).astype(jnp.float32)
        weight_rows = lax.optimization_barrier(jnp.sum(jnp.where(matches, gate_values, 0.0), axis=1))[row_index]
        combined = combined.at[row_index].add(weight_rows[:, None] * expert_out)
    return (hidden_state + combined).astype(jnp.bfloat16).reshape(PACKET_TRACES, NEW_POSITIONS, D)
```

```python
import functools
import math

import jax
import jax.numpy as jnp
from jax import lax
from jax.experimental import pallas as pl
from jax.experimental.pallas import tpu as pltpu
from jax.sharding import PartitionSpec as P

EPSILON = 1e-05
NEGATIVE = -1e30
SIDE = 4
CORES = 2
BF16 = jnp.bfloat16
F32 = jnp.float32
NT = (((1,), (1,)), ((), ()))


def ctx_id(x, y, core):
    return ((x % SIDE) * SIDE + y % SIDE) * CORES + core


def ring_pairs(phase, step):
    pairs = []
    for x in range(SIDE):
        for y in range(SIDE):
            for core in range(CORES):
                dx, dy = (step, 0) if phase == core else (0, step)
                pairs.append((ctx_id(x, y, core), ctx_id(x + dx, y + dy, core)))
    return pairs


SWAP = [(i, i ^ 1) for i in range(SIDE * SIDE * CORES)]
ORDER = (0, -1, 1, 2)


def move(value, phase, step):
    return lax.ppermute(value, "ctx", ring_pairs(phase, step))


def swap(value):
    return lax.ppermute(value, "ctx", SWAP)


def z_move(value, step):
    count = lax.axis_size("exp")
    pairs = []
    for device in range(SIDE * SIDE * CORES):
        way = step if device % CORES == 0 else -step
        pairs += [(device * count + z, device * count + (z + way) % count) for z in range(count)]
    return lax.ppermute(value, ("ctx", "exp"), pairs)


def z_shift(value, step):
    count = lax.axis_size("exp")
    return lax.ppermute(value, "exp", [(z, (z + step) % count) for z in range(count)])


def add16(a, b):
    return (a.astype(F32) + b.astype(F32)).astype(BF16)


def near_gather(block, phase):
    return {0: block, -1: move(block, phase, 1), 1: move(block, phase, -1)}


def far_gather(blocks, phase):
    half = blocks[0].shape[1] // 2
    left, right = blocks[-1][:, :half], blocks[1][:, half:]
    return jnp.concatenate((move(left, phase, 1), move(right, phase, -1)), axis=1)


def ring_gather(block, phase):
    blocks = near_gather(block, phase)
    blocks[2] = far_gather(blocks, phase)
    return blocks


def ring_sum(left, right, phase, joined):
    half = left[0].shape[1]
    if joined:
        up = move(jnp.concatenate((left[2], right[1]), axis=1), phase, 1)
        down = move(jnp.concatenate((left[-1], right[2]), axis=1), phase, -1)
        far_up, near_up = up[:, :half], up[:, half:]
        near_down, far_down = down[:, :half], down[:, half:]
    else:
        near_up, near_down = move(right[1], phase, 1), move(left[-1], phase, -1)
        far_up, far_down = move(left[2], phase, 1), move(right[2], phase, -1)
    up_on = move(add16(left[1], far_up), phase, 1)
    down_on = move(add16(right[-1], far_down), phase, -1)
    return (
        left[0].astype(F32) + up_on.astype(F32) + near_down.astype(F32),
        right[0].astype(F32) + down_on.astype(F32) + near_up.astype(F32),
    )


def attend_kernel(first, last, scale, shard, cached, *refs):
    if first:
        key_base, query_base, q_ref, kv_ref = refs[:4]
        rest = refs[4:]
    else:
        key_base, query_base, q_ref, kv_ref, max_in, sum_in, acc_in = refs[:7]
        rest = refs[7:]
    if last:
        out_ref, q_s, max_s, sum_s, acc_s = rest
    else:
        max_s, sum_s, acc_s, q_s = rest
    positions, width = q_ref.shape
    head = 128
    heads = width // head
    rows = positions * heads
    for h in range(heads):
        q_s[h * positions : (h + 1) * positions, :] = q_ref[:, h * head : (h + 1) * head]
    if first:
        max_s[...] = jnp.full_like(max_s, NEGATIVE)
        sum_s[...] = jnp.zeros_like(sum_s)
        acc_s[...] = jnp.zeros_like(acc_s)
    else:
        max_s[...] = max_in[...]
        sum_s[...] = sum_in[...]
        acc_s[...] = acc_in[...]
    fresh = shard - cached
    column = lax.broadcasted_iota(jnp.int32, (rows, fresh), 1)
    ahead = column - lax.broadcasted_iota(jnp.int32, (rows, fresh), 0) % positions

    @pl.loop(0, kv_ref.shape[0] // shard)
    def _(step):
        start = pl.multiple_of(step * shard, shard)
        keys = kv_ref[pl.ds(start, shard), :head]
        values = kv_ref[pl.ds(start, shard), head:]
        room = query_base[0] - key_base[step]
        raw = lax.dot_general(q_s[...], keys, NT, preferred_element_type=F32)
        late = jnp.where(ahead <= room, raw[:, cached:], NEGATIVE)
        parts = [raw[:, i * head : (i + 1) * head] for i in range(cached // head)]
        parts += [late[:, i * head : (i + 1) * head] for i in range(fresh // head)]
        old = max_s[:, :1]
        top = jnp.max(functools.reduce(jnp.maximum, parts), axis=1, keepdims=True)
        new = jnp.maximum(old, top * scale)
        shrink = jnp.exp2(old - new)
        weights = [jnp.exp2(part * scale - new) for part in parts]
        sum_s[...] = sum_s[...] * shrink + functools.reduce(jnp.add, weights)
        mixed = jnp.concatenate([part.astype(BF16) for part in weights], axis=1)
        acc_s[...] = acc_s[...] * shrink + jnp.dot(mixed, values, preferred_element_type=F32)
        max_s[...] = jnp.broadcast_to(new, max_s.shape)

    if last:
        total = jnp.sum(sum_s[...], axis=1, keepdims=True)
        mixed = (acc_s[...] / total).astype(BF16)
        for h in range(heads):
            out_ref[:, h * head : (h + 1) * head] = mixed[h * positions : (h + 1) * positions, :]


def attend(query_rows, kv_rows, key_base, query_base, state, last, shard, cached):
    positions, width = query_rows.shape
    head = 128
    rows = positions * width // head
    first = state is None
    scale = math.log2(math.e) / math.sqrt(head)
    shape = jax.ShapeDtypeStruct((rows, head), F32)
    vmem = pl.BlockSpec(memory_space=pltpu.VMEM)
    smem = pl.BlockSpec(memory_space=pltpu.SMEM)
    operands = (key_base, query_base, query_rows, kv_rows) + (() if first else tuple(state))
    keys = kv_rows.shape[0]
    scratch = [pltpu.VMEM((rows, head), BF16)]
    return pl.pallas_call(
        functools.partial(attend_kernel, first, last, scale, shard, cached),
        out_shape=jax.ShapeDtypeStruct((positions, width), BF16) if last else (shape,) * 3,
        in_specs=[smem, smem] + [vmem] * (len(operands) - 2),
        out_specs=vmem if last else (vmem,) * 3,
        scratch_shapes=scratch + ([pltpu.VMEM((rows, head), F32)] * 3 if last else []),
        compiler_params=pltpu.CompilerParams(vmem_limit_bytes=32 << 20),
        cost_estimate=pl.CostEstimate(
            flops=4 * rows * keys * head, bytes_accessed=keys * 512, transcendentals=rows * keys
        ),
    )(*operands)


def stack(blocks):
    return jnp.concatenate([blocks[d] for d in ORDER], axis=0)


def on_device(
    residual,
    queries,
    cache_kv,
    fresh_key_value,
    out_weight,
    norm_gain,
    router_weight,
    gate_weight,
    up_weight,
    down_weight,
    expert_ids,
):
    new_local = queries.shape[1]
    exp_count = lax.axis_size("exp")
    model_width = out_weight.shape[1]
    width = model_width // exp_count
    half = width // 2
    own_tokens = 2 * new_local
    ctx_index = lax.axis_index("ctx")
    z = lax.axis_index("exp")
    core = ctx_index % CORES
    lead = core == 0
    way = 1 - 2 * core
    chip_x = ctx_index // (CORES * SIDE)
    chip_y = ctx_index // CORES % SIDE

    def by_core(own, other, axis=0):
        return jnp.concatenate((jnp.where(lead, own, other), jnp.where(lead, other, own)), axis=axis)

    def mine(value):
        return jnp.where(lead, value[0], value[1])

    def theirs(value):
        return jnp.where(lead, value[1], value[0])

    cache_rows = jnp.concatenate((cache_kv[0], cache_kv[1]), axis=2)
    fresh_rows = jnp.concatenate((fresh_key_value[0], fresh_key_value[1]), axis=2)
    sent = swap(jnp.concatenate((theirs(cache_rows), theirs(fresh_rows)), axis=0))
    cached = cache_rows.shape[1]
    kv_block = jnp.concatenate(
        (by_core(mine(cache_rows), sent[:cached]), by_core(mine(fresh_rows), sent[cached:])), axis=0
    )
    shard = kv_block.shape[0]
    query_rows = by_core(mine(queries), swap(theirs(queries)))
    positions = query_rows.shape[0]
    query_base = ((chip_x * SIDE + chip_y) * positions).reshape(1).astype(jnp.int32)

    def key_base(distances):
        chips = []
        for far in distances:
            for near in ORDER:
                dx, dy = jnp.where(lead, near, far), jnp.where(lead, far, near)
                chips.append(ctx_id(chip_x + dx + SIDE, chip_y + dy + SIDE, 0) // CORES)
        return (jnp.stack(chips) * positions).astype(jnp.int32)

    gate_own, up_own, down_own = gate_weight[0].T, up_weight[0].T, down_weight[0]
    gate_other, up_other, down_other = swap(gate_own), swap(up_own), swap(down_own)
    hidden_units = 2 * gate_own.shape[0]
    residual_own = residual.reshape(own_tokens, width)
    picked_own = jnp.transpose(expert_ids, (1, 0, 2)).reshape(own_tokens, 2)
    picked_all = by_core(picked_own, swap(picked_own))

    line = ring_gather(kv_block, 0)
    rows_near = stack(line)
    blocks = near_gather(rows_near, 1)
    query_rows, gate_other, up_other, down_other = lax.optimization_barrier(
        (query_rows, gate_other, up_other, down_other)
    )
    state = attend(query_rows, rows_near, key_base((0,)), query_base, None, False, shard, 2 * cached)
    blocks[-1], blocks[1], state = lax.optimization_barrier((blocks[-1], blocks[1], state))
    far = far_gather(blocks, 1)
    rows_mid = jnp.concatenate((blocks[-1], blocks[1]), axis=0)
    state = attend(query_rows, rows_mid, key_base((-1, 1)), query_base, state, False, shard, 2 * cached)
    attended = attend(query_rows, far, key_base((2,)), query_base, state, True, shard, 2 * cached)

    ours, others = attended[:new_local], attended[new_local:]
    ours, others = jnp.where(lead, ours, others), jnp.where(lead, others, ours)
    heads = by_core(ours, swap(others))

    product = jnp.dot(heads, out_weight, preferred_element_type=F32)
    product, gate_other, up_other = lax.optimization_barrier((product, gate_other, up_other))
    wide = jnp.concatenate((gate_own, gate_other, up_own, up_other), axis=0)

    def share(distance):
        column = (z + distance + exp_count) % exp_count * width
        return lax.dynamic_slice_in_dim(product, column, width, 1)

    top = exp_count // 2
    opposite = share(top)
    up = jnp.concatenate((share(3), opposite[:, :half]), axis=1).astype(BF16)
    down = jnp.concatenate((share(-3), opposite[:, half:]), axis=1).astype(BF16)
    up, down = z_shift(up, 2), z_shift(down, -2)
    up, down, wide, down_other = lax.optimization_barrier((up, down, wide, down_other))
    up, down = up.astype(F32), down.astype(F32)
    middle = model_width // 2
    down_left = jnp.concatenate((down_own[:, :middle], down_other[:, :middle]), axis=0)
    down_right = jnp.concatenate((down_own[:, middle:], down_other[:, middle:]), axis=0)
    nothing = jnp.zeros_like(opposite[:, :half])
    up_two = share(2) + jnp.concatenate((up[:, width:], nothing), axis=1)
    down_two = share(-2) + jnp.concatenate((nothing, down[:, width:]), axis=1)
    up_one, down_one = share(1) + up[:, :width], share(-1) + down[:, :width]
    arrived = (
        z_shift(up_two.astype(BF16), 2),
        z_shift(down_two.astype(BF16), -2),
        z_shift(up_one.astype(BF16), 1),
        z_shift(down_one.astype(BF16), -1),
    )
    arrived, down_left, down_right = lax.optimization_barrier((arrived, down_left, down_right))
    hidden_own = share(0) + residual_own.astype(F32)
    for value in arrived:
        hidden_own = hidden_own + value.astype(F32)
    hidden16 = hidden_own.astype(BF16)
    hidden16 = by_core(hidden16, swap(hidden16)).reshape(CORES, own_tokens, width)

    capacity = own_tokens * 2 // exp_count
    experts = jnp.arange(exp_count, dtype=jnp.int32)
    named = jnp.any(picked_all[:, :, None] == experts, axis=1).reshape(CORES, own_tokens, exp_count)
    order = jnp.cumsum(named.astype(jnp.int32), axis=1) - 1
    named, order = jnp.transpose(named, (0, 2, 1)), jnp.transpose(order, (0, 2, 1))
    slots = jnp.arange(capacity, dtype=jnp.int32)[None, None, :, None]
    chosen = named[:, :, None, :] & (order[:, :, None, :] == slots)
    selector = chosen.reshape(CORES, exp_count * capacity, own_tokens).astype(BF16)
    chosen_own = jnp.where(lead, chosen[0], chosen[1])
    selector_own = jnp.where(lead, selector[0], selector[1])

    def exchange(pieces):
        def to(distance):
            index = (z + way * distance + exp_count) % exp_count
            return lax.dynamic_index_in_dim(pieces, index, 0, keepdims=False)

        came = [z_move(to(distance), distance) for distance in range(1, top)]
        opposite = to(top)
        came.append(z_move(jnp.where(lead, opposite[:, :half], opposite[:, half:]), top))
        came = jnp.concatenate(came, axis=1)
        keep = jnp.where(lead, came[:capacity], came[capacity:])
        give = swap(jnp.where(lead, came[capacity:], came[:capacity]))
        low, high = jnp.where(lead, keep, give), jnp.where(lead, give, keep)
        here = to(0)
        here = jnp.where(lead, here[:capacity], here[capacity:])
        cut = [slice(i * width, (i + 1) * width) for i in range(top - 1)]
        rest = slice((top - 1) * width, None)
        ahead = [high[:, c] for c in cut]
        behind = [low[:, c] for c in cut][::-1]
        across = jnp.concatenate((low[:, rest], high[:, rest]), axis=1)
        around = jnp.stack([here] + ahead + [across] + behind, axis=0)
        return jnp.roll(around, z, axis=0)

    rows = jnp.einsum("cst,ctf->csf", selector, hidden16, preferred_element_type=F32).astype(BF16)
    rows = rows.reshape(CORES, exp_count, capacity, width)
    rows = exchange(jnp.concatenate((rows[0], rows[1]), axis=1))
    rows = jnp.transpose(rows, (1, 0, 2)).reshape(capacity, model_width).astype(F32)
    normed = (
        rows * lax.rsqrt(jnp.mean(rows * rows, axis=1, keepdims=True) + EPSILON) * norm_gain
    ).astype(BF16)

    logits = jnp.dot(normed, router_weight, preferred_element_type=F32)
    own_slots = lax.dynamic_index_in_dim(chosen_own, z, 0, keepdims=False)
    other_id = jnp.sum(picked_own, axis=1) - z
    other_of_row = jnp.sum(jnp.where(own_slots, other_id[None, :], 0), axis=1)
    own_logit = jnp.sum(jnp.where(experts[None, :] == z, logits, 0.0), axis=1)
    other_logit = jnp.sum(jnp.where(experts[None, :] == other_of_row[:, None], logits, 0.0), axis=1)
    gate_values = jax.nn.sigmoid(own_logit - other_logit)

    def expert(block):
        both = lax.dot_general(block, wide, NT, preferred_element_type=F32)
        active = (jax.nn.silu(both[:, :hidden_units]) * both[:, hidden_units:]).astype(BF16)
        return [
            jnp.dot(active, down, preferred_element_type=F32).astype(BF16)
            for down in (down_left, down_right)
        ]

    token_line = stack(ring_gather(normed, 0))
    count = token_line.shape[0]
    blocks = near_gather(token_line, 1)
    left, right = {}, {}
    left[0], right[0] = expert(token_line)
    blocks[-1], blocks[1], left[0], right[0] = lax.optimization_barrier(
        (blocks[-1], blocks[1], left[0], right[0])
    )
    far = far_gather(blocks, 1)
    near_left, near_right = expert(jnp.concatenate((blocks[-1], blocks[1]), axis=0))
    left[-1], left[1] = near_left[:count], near_left[count:]
    right[-1], right[1] = near_right[:count], near_right[count:]
    left[2], right[2] = expert(far)
    line = ring_sum(left, right, 1, False)
    line = lax.optimization_barrier([value.astype(BF16) for value in line])
    left, right = [
        {d: value[i * capacity : (i + 1) * capacity] for i, d in enumerate(ORDER)} for value in line
    ]
    returned = jnp.concatenate(ring_sum(left, right, 0, True), axis=1).astype(BF16).astype(F32)

    scaled = (gate_values[:, None] * returned).astype(BF16)

    def pick(distance, start=0, size=width):
        column = (z + distance + exp_count) % exp_count * width + start
        return lax.dynamic_slice_in_dim(scaled, column, size, 1)

    for_other = [pick(-way * distance) for distance in range(1, top)]
    for_other = jnp.concatenate(for_other + [pick(top, (1 - core) * half, half)], axis=1)
    for_this = [pick(way * distance) for distance in range(1, top)]
    for_this = jnp.concatenate(for_this + [pick(top, core * half, half)], axis=1)
    both = by_core(for_this, swap(for_other))
    came = [
        z_move(both[:, (distance - 1) * width : distance * width], distance)
        for distance in range(1, top + 1)
    ]
    came = jnp.concatenate(came, axis=1)
    keep = jnp.where(lead, came[:capacity], came[capacity:])
    give = swap(jnp.where(lead, came[capacity:], came[:capacity]))
    low, high = jnp.where(lead, keep, give), jnp.where(lead, give, keep)
    cut = [slice(i * width, (i + 1) * width) for i in range(top - 1)]
    rest = slice((top - 1) * width, None)
    across = jnp.concatenate((low[:, rest], high[:, rest]), axis=1)
    around = [pick(0)] + [high[:, c] for c in cut] + [across] + [low[:, c] for c in cut][::-1]
    home = jnp.roll(jnp.stack(around, axis=0), z, axis=0).reshape(exp_count * capacity, width)
    merged = lax.dot_general(
        selector_own, home, (((0,), (0,)), ((), ())), preferred_element_type=F32
    )
    return (hidden_own + merged).astype(BF16).reshape(2, new_local, width)


def solution(mesh):
    placed = (
        P(None, "ctx", "exp"),
        P(None, "ctx", "exp"),
        P(None, None, "ctx", "exp"),
        P(None, None, "ctx", "exp"),
        P("exp", None),
        P(),
        P(),
        P("exp", None, "ctx"),
        P("exp", None, "ctx"),
        P("exp", "ctx", None),
        P("ctx", None, None),
    )
    return jax.shard_map(
        on_device, mesh=mesh, in_specs=placed, out_specs=P(None, "ctx", "exp"), check_vma=False
    )
```

```python
import functools
import math

import jax
import jax.numpy as jnp
from jax import lax
from jax.experimental import pallas as pl
from jax.experimental.pallas import tpu as pltpu
from jax.sharding import PartitionSpec as P

EPSILON = 1e-05
NEGATIVE = -1e30
SIDE = 4
CORES = 2
BF16 = jnp.bfloat16
F32 = jnp.float32
NT = (((1,), (1,)), ((), ()))


def ctx_id(x, y, core):
    return ((x % SIDE) * SIDE + y % SIDE) * CORES + core


def ring_pairs(phase, step):
    pairs = []
    for x in range(SIDE):
        for y in range(SIDE):
            for core in range(CORES):
                dx, dy = (step, 0) if phase == core else (0, step)
                pairs.append((ctx_id(x, y, core), ctx_id(x + dx, y + dy, core)))
    return pairs


SWAP = [(i, i ^ 1) for i in range(SIDE * SIDE * CORES)]
ORDER = (0, -1, 1, 2)


def move(value, phase, step):
    return lax.ppermute(value, "ctx", ring_pairs(phase, step))


def swap(value):
    return lax.ppermute(value, "ctx", SWAP)


def z_move(value, step):
    count = lax.axis_size("exp")
    pairs = []
    for device in range(SIDE * SIDE * CORES):
        way = step if device % CORES == 0 else -step
        pairs += [(device * count + z, device * count + (z + way) % count) for z in range(count)]
    return lax.ppermute(value, ("ctx", "exp"), pairs)


def z_shift(value, step):
    count = lax.axis_size("exp")
    return lax.ppermute(value, "exp", [(z, (z + step) % count) for z in range(count)])


def add16(a, b):
    return (a.astype(F32) + b.astype(F32)).astype(BF16)


def near_gather(block, phase):
    return {0: block, -1: move(block, phase, 1), 1: move(block, phase, -1)}


def far_gather(blocks, phase):
    half = blocks[0].shape[1] // 2
    left, right = blocks[-1][:, :half], blocks[1][:, half:]
    return jnp.concatenate((move(left, phase, 1), move(right, phase, -1)), axis=1)


def small_gather(block, phase):
    far = move(block, phase, 2)
    blocks = near_gather(block, phase)
    blocks[2] = far
    return blocks


def small_sum(parts, phase):
    came = [move(parts[2], phase, 2), move(parts[1], phase, 1), move(parts[-1], phase, -1)]
    return sum([value.astype(F32) for value in came], parts[0].astype(F32))


def ring_sum(parts, phase):
    half = parts[0].shape[1] // 2
    near_up, near_down = move(parts[1][:, half:], phase, 1), move(parts[-1][:, :half], phase, -1)
    far_up, far_down = move(parts[2][:, :half], phase, 1), move(parts[2][:, half:], phase, -1)
    up_on, down_on = lax.optimization_barrier(
        (add16(parts[1][:, :half], far_up), add16(parts[-1][:, half:], far_down))
    )
    up_on, down_on = move(up_on, phase, 1), move(down_on, phase, -1)
    left = parts[0][:, :half].astype(F32) + up_on.astype(F32) + near_down.astype(F32)
    right = parts[0][:, half:].astype(F32) + down_on.astype(F32) + near_up.astype(F32)
    return left, right


def attend_kernel(first, last, scale, shard, cached, *refs):
    if first:
        key_base, query_base, q_ref, kv_ref = refs[:4]
        rest = refs[4:]
    else:
        key_base, query_base, q_ref, kv_ref, max_in, sum_in, acc_in = refs[:7]
        rest = refs[7:]
    if last:
        out_ref, q_s, max_s, sum_s, acc_s = rest
    else:
        max_s, sum_s, acc_s, q_s = rest
    positions, width = q_ref.shape
    head = 128
    heads = width // head
    rows = positions * heads
    for h in range(heads):
        q_s[h * positions : (h + 1) * positions, :] = q_ref[:, h * head : (h + 1) * head]
    if first:
        max_s[...] = jnp.full_like(max_s, NEGATIVE)
        sum_s[...] = jnp.zeros_like(sum_s)
        acc_s[...] = jnp.zeros_like(acc_s)
    else:
        max_s[...] = max_in[...]
        sum_s[...] = sum_in[...]
        acc_s[...] = acc_in[...]
    fresh = shard - cached
    column = lax.broadcasted_iota(jnp.int32, (rows, fresh), 1)
    ahead = column - lax.broadcasted_iota(jnp.int32, (rows, fresh), 0) % positions

    @pl.loop(0, kv_ref.shape[0] // shard)
    def _(step):
        start = pl.multiple_of(step * shard, shard)
        keys = kv_ref[pl.ds(start, shard), :head]
        values = kv_ref[pl.ds(start, shard), head:]
        room = query_base[0] - key_base[step]
        raw = lax.dot_general(q_s[...], keys, NT, preferred_element_type=F32)
        late = jnp.where(ahead <= room, raw[:, cached:], NEGATIVE)
        parts = [raw[:, i * head : (i + 1) * head] for i in range(cached // head)]
        parts += [late[:, i * head : (i + 1) * head] for i in range(fresh // head)]
        old = max_s[:, :1]
        top = jnp.max(functools.reduce(jnp.maximum, parts), axis=1, keepdims=True)
        new = jnp.maximum(old, top * scale)
        shrink = jnp.exp2(old - new)
        weights = [jnp.exp2(part * scale - new) for part in parts]
        sum_s[...] = sum_s[...] * shrink + functools.reduce(jnp.add, weights)
        mixed = jnp.concatenate([part.astype(BF16) for part in weights], axis=1)
        acc_s[...] = acc_s[...] * shrink + jnp.dot(mixed, values, preferred_element_type=F32)
        max_s[...] = jnp.broadcast_to(new, max_s.shape)

    if last:
        total = jnp.sum(sum_s[...], axis=1, keepdims=True)
        mixed = (acc_s[...] / total).astype(BF16)
        for h in range(heads):
            out_ref[:, h * head : (h + 1) * head] = mixed[h * positions : (h + 1) * positions, :]


def attend(query_rows, kv_rows, key_base, query_base, state, last, shard, cached):
    positions, width = query_rows.shape
    head = 128
    rows = positions * width // head
    first = state is None
    scale = math.log2(math.e) / math.sqrt(head)
    shape = jax.ShapeDtypeStruct((rows, head), F32)
    vmem = pl.BlockSpec(memory_space=pltpu.VMEM)
    smem = pl.BlockSpec(memory_space=pltpu.SMEM)
    operands = (key_base, query_base, query_rows, kv_rows) + (() if first else tuple(state))
    keys = kv_rows.shape[0]
    scratch = [pltpu.VMEM((rows, head), BF16)]
    return pl.pallas_call(
        functools.partial(attend_kernel, first, last, scale, shard, cached),
        out_shape=jax.ShapeDtypeStruct((positions, width), BF16) if last else (shape,) * 3,
        in_specs=[smem, smem] + [vmem] * (len(operands) - 2),
        out_specs=vmem if last else (vmem,) * 3,
        scratch_shapes=scratch + ([pltpu.VMEM((rows, head), F32)] * 3 if last else []),
        compiler_params=pltpu.CompilerParams(vmem_limit_bytes=32 << 20),
        cost_estimate=pl.CostEstimate(
            flops=4 * rows * keys * head, bytes_accessed=keys * 512, transcendentals=rows * keys
        ),
    )(*operands)


def stack(blocks):
    return jnp.concatenate([blocks[d] for d in ORDER], axis=0)


def on_device(
    residual,
    queries,
    cache_kv,
    fresh_key_value,
    out_weight,
    norm_gain,
    router_weight,
    gate_weight,
    up_weight,
    down_weight,
    expert_ids,
):
    new_local = queries.shape[1]
    exp_count = lax.axis_size("exp")
    model_width = out_weight.shape[1]
    width = model_width // exp_count
    half = width // 2
    own_tokens = 2 * new_local
    ctx_index = lax.axis_index("ctx")
    z = lax.axis_index("exp")
    core = ctx_index % CORES
    lead = core == 0
    way = 1 - 2 * core
    chip_x = ctx_index // (CORES * SIDE)
    chip_y = ctx_index // CORES % SIDE

    def by_core(own, other, axis=0):
        return jnp.concatenate((jnp.where(lead, own, other), jnp.where(lead, other, own)), axis=axis)

    def mine(value):
        return jnp.where(lead, value[0], value[1])

    def theirs(value):
        return jnp.where(lead, value[1], value[0])

    cache_rows = jnp.concatenate((cache_kv[0], cache_kv[1]), axis=2)
    fresh_rows = jnp.concatenate((fresh_key_value[0], fresh_key_value[1]), axis=2)
    sent = swap(jnp.concatenate((theirs(cache_rows), theirs(fresh_rows)), axis=0))
    cached = cache_rows.shape[1]
    kv_block = jnp.concatenate(
        (by_core(mine(cache_rows), sent[:cached]), by_core(mine(fresh_rows), sent[cached:])), axis=0
    )
    shard = kv_block.shape[0]
    query_rows = by_core(mine(queries), swap(theirs(queries)))
    positions = query_rows.shape[0]
    query_base = ((chip_x * SIDE + chip_y) * positions).reshape(1).astype(jnp.int32)

    def key_base(distances):
        chips = []
        for far in distances:
            for near in ORDER:
                dx, dy = jnp.where(lead, near, far), jnp.where(lead, far, near)
                chips.append(ctx_id(chip_x + dx + SIDE, chip_y + dy + SIDE, 0) // CORES)
        return (jnp.stack(chips) * positions).astype(jnp.int32)

    gate_own, up_own, down_own = gate_weight[0].T, up_weight[0].T, down_weight[0]
    residual_own = residual.reshape(own_tokens, width)
    picked_own = jnp.transpose(expert_ids, (1, 0, 2)).reshape(own_tokens, 2)

    line = small_gather(kv_block, 0)
    line[2], gate_sent, up_sent, down_sent = lax.optimization_barrier(
        (line[2], gate_own, up_own, down_own)
    )
    gate_other, up_other, down_other = swap(gate_sent), swap(up_sent), swap(down_sent)
    rows_near = stack(line)
    blocks = near_gather(rows_near, 1)
    state = attend(query_rows, rows_near, key_base((0,)), query_base, None, False, shard, 2 * cached)
    blocks[-1], blocks[1], state = lax.optimization_barrier((blocks[-1], blocks[1], state))
    far = far_gather(blocks, 1)
    rows_mid = jnp.concatenate((blocks[-1], blocks[1]), axis=0)
    state = attend(query_rows, rows_mid, key_base((-1, 1)), query_base, state, False, shard, 2 * cached)
    query_rows, gate_other, up_other, down_other = lax.optimization_barrier(
        (query_rows, gate_other, up_other, down_other)
    )
    attended = attend(query_rows, far, key_base((2,)), query_base, state, True, shard, 2 * cached)

    ours, others = attended[:new_local], attended[new_local:]
    ours, others = jnp.where(lead, ours, others), jnp.where(lead, others, ours)
    heads = by_core(ours, swap(others))

    capacity = own_tokens * 2 // exp_count
    experts = jnp.arange(exp_count, dtype=jnp.int32)
    named = jnp.any(picked_own[:, :, None] == experts, axis=1)
    order = jnp.cumsum(named.astype(jnp.int32), axis=0) - 1
    slots = jnp.arange(capacity, dtype=jnp.int32)
    chosen = named.T[:, None, :] & (order.T[:, None, :] == slots[None, :, None])
    selector = chosen.reshape(exp_count * capacity, own_tokens).astype(BF16)

    chosen_heads = jnp.dot(selector, heads, preferred_element_type=F32).astype(BF16)
    chosen_residual = jnp.dot(selector, residual_own, preferred_element_type=F32)
    product = jnp.dot(chosen_heads, out_weight, preferred_element_type=F32).astype(BF16)
    here = lax.dynamic_slice_in_dim(out_weight, z * width, width, 1)
    here = jnp.dot(chosen_heads, here, preferred_element_type=F32) + chosen_residual
    product = lax.dynamic_update_slice_in_dim(product, here.astype(BF16), z * width, 1)
    product = product.reshape(exp_count, capacity, model_width)

    def share(distance):
        index = (z + distance + exp_count) % exp_count
        return lax.dynamic_index_in_dim(product, index, 0, keepdims=False).astype(F32)

    top = exp_count // 2
    middle = model_width // 2
    opposite = share(top).astype(BF16)
    up, down = z_shift(opposite[:, :middle], 1), z_shift(opposite[:, middle:], -1)
    up_share, down_share = share(top - 1), share(1 - top)
    up = jnp.concatenate((up_share[:, :middle] + up.astype(F32), up_share[:, middle:]), axis=1)
    down = jnp.concatenate(
        (down_share[:, :middle], down_share[:, middle:] + down.astype(F32)), axis=1
    )
    gate_other = lax.optimization_barrier((gate_other, product))[0]
    waiting = [(gate_own, gate_other), (up_own, up_other), (down_own, down_other)]
    pairs = []
    for distance in range(top - 1, 0, -1):
        pair = jnp.concatenate(waiting[len(pairs)], axis=0)
        up, down = lax.optimization_barrier((up.astype(BF16), down.astype(BF16)))
        up, down = z_shift(up, 1), z_shift(down, -1)
        up, down, pair = lax.optimization_barrier((up, down, pair))
        pairs.append(pair)
        if len(pairs) < len(waiting):
            own, other = waiting[len(pairs)]
            waiting[len(pairs)] = (own, lax.optimization_barrier((other, up))[0])
        up, down = up.astype(F32), down.astype(F32)
        if distance > 1:
            up, down = up + share(distance - 1), down + share(1 - distance)
    gate_both, up_both, down_both = pairs
    rows = share(0) + up + down
    normed = (
        rows * lax.rsqrt(jnp.mean(rows * rows, axis=1, keepdims=True) + EPSILON) * norm_gain
    ).astype(BF16)

    logits = jnp.dot(normed, router_weight, preferred_element_type=F32)
    own_slots = lax.dynamic_index_in_dim(chosen, z, 0, keepdims=False)
    other_id = jnp.sum(picked_own, axis=1) - z
    other_of_row = jnp.sum(jnp.where(own_slots, other_id[None, :], 0), axis=1)
    own_logit = jnp.sum(jnp.where(experts[None, :] == z, logits, 0.0), axis=1)
    other_logit = jnp.sum(jnp.where(experts[None, :] == other_of_row[:, None], logits, 0.0), axis=1)
    gate_values = jax.nn.sigmoid(own_logit - other_logit)
    first = jnp.any(own_slots & (picked_own[:, 0] == z)[None, :], axis=1)

    def expert(block):
        gate = lax.dot_general(block, gate_both, NT, preferred_element_type=F32)
        active = lax.dot_general(block, up_both, NT, preferred_element_type=F32)
        gate, active = lax.optimization_barrier((gate, active))
        active = (jax.nn.silu(gate) * active).astype(BF16)
        return jnp.dot(active, down_both, preferred_element_type=F32).astype(BF16)

    token_line = stack(small_gather(normed, 0))
    count = token_line.shape[0]
    blocks = near_gather(token_line, 1)
    parts = {0: expert(token_line)}
    blocks[-1], blocks[1], parts[0] = lax.optimization_barrier((blocks[-1], blocks[1], parts[0]))
    far = far_gather(blocks, 1)
    near = expert(jnp.concatenate((blocks[-1], blocks[1]), axis=0))
    far, near = lax.optimization_barrier((far, near))
    parts[-1], parts[1] = near[:count], near[count:]
    parts[2] = lax.optimization_barrier(expert(far))
    line = [value.astype(BF16) for value in ring_sum(parts, 1)]
    line = jnp.concatenate(lax.optimization_barrier(line), axis=1)
    line = lax.optimization_barrier(line)
    returned = small_sum(
        {d: line[i * capacity : (i + 1) * capacity] for i, d in enumerate(ORDER)}, 0
    )
    returned = returned.astype(BF16).astype(F32)

    scaled = gate_values[:, None] * returned + jnp.where(first[:, None], rows, 0.0)
    scaled = scaled.astype(BF16)

    def pick(distance, start=0, size=width):
        column = (z + distance + exp_count) % exp_count * width + start
        return lax.dynamic_slice_in_dim(scaled, column, size, 1)

    for_other = [pick(-way * distance) for distance in range(1, top)]
    for_other = jnp.concatenate(for_other + [pick(top, (1 - core) * half, half)], axis=1)
    for_this = [pick(way * distance) for distance in range(1, top)]
    for_this = jnp.concatenate(for_this + [pick(top, core * half, half)], axis=1)
    both = by_core(for_this, swap(for_other))
    came = [
        z_move(both[:, (distance - 1) * width : distance * width], distance)
        for distance in range(1, top + 1)
    ]
    came = jnp.concatenate(came, axis=1)
    keep = jnp.where(lead, came[:capacity], came[capacity:])
    give = swap(jnp.where(lead, came[capacity:], came[:capacity]))
    low, high = jnp.where(lead, keep, give), jnp.where(lead, give, keep)
    cut = [slice(i * width, (i + 1) * width) for i in range(top - 1)]
    rest = slice((top - 1) * width, None)
    across = jnp.concatenate((low[:, rest], high[:, rest]), axis=1)
    around = [pick(0)] + [high[:, c] for c in cut] + [across] + [low[:, c] for c in cut][::-1]
    home = jnp.roll(jnp.stack(around, axis=0), z, axis=0).reshape(exp_count * capacity, width)
    result = lax.dot_general(selector, home, (((0,), (0,)), ((), ())), preferred_element_type=F32)
    return result.astype(BF16).reshape(2, new_local, width)


def solution(mesh):
    placed = (
        P(None, "ctx", "exp"),
        P(None, "ctx", "exp"),
        P(None, None, "ctx", "exp"),
        P(None, None, "ctx", "exp"),
        P("exp", None),
        P(),
        P(),
        P("exp", None, "ctx"),
        P("exp", None, "ctx"),
        P("exp", "ctx", None),
        P("ctx", None, None),
    )
    return jax.shard_map(
        on_device, mesh=mesh, in_specs=placed, out_specs=P(None, "ctx", "exp"), check_vma=False
    )
```

```python
import functools
import math

import jax
import jax.numpy as jnp
from jax import lax
from jax.experimental import pallas as pl
from jax.experimental.pallas import tpu as pltpu
from jax.sharding import PartitionSpec as P

EPSILON = 1e-05
NEGATIVE = -1e30
SIDE = 4
CORES = 2
BF16 = jnp.bfloat16
F32 = jnp.float32
NT = (((1,), (1,)), ((), ()))


def ctx_id(x, y, core):
    return ((x % SIDE) * SIDE + y % SIDE) * CORES + core


def ring_pairs(phase, step):
    pairs = []
    for x in range(SIDE):
        for y in range(SIDE):
            for core in range(CORES):
                dx, dy = (step, 0) if phase == core else (0, step)
                pairs.append((ctx_id(x, y, core), ctx_id(x + dx, y + dy, core)))
    return pairs


SWAP = [(i, i ^ 1) for i in range(SIDE * SIDE * CORES)]
ORDER = (0, -1, 1, 2)


def move(value, phase, step):
    return lax.ppermute(value, "ctx", ring_pairs(phase, step))


def swap(value):
    return lax.ppermute(value, "ctx", SWAP)


def z_move(value, step):
    count = lax.axis_size("exp")
    pairs = []
    for device in range(SIDE * SIDE * CORES):
        way = step if device % CORES == 0 else -step
        pairs += [(device * count + z, device * count + (z + way) % count) for z in range(count)]
    return lax.ppermute(value, ("ctx", "exp"), pairs)


def add16(a, b):
    return (a.astype(F32) + b.astype(F32)).astype(BF16)


def near_gather(block, phase):
    return {0: block, -1: move(block, phase, 1), 1: move(block, phase, -1)}


def far_gather(blocks, phase):
    half = blocks[0].shape[1] // 2
    left, right = blocks[-1][:, :half], blocks[1][:, half:]
    return jnp.concatenate((move(left, phase, 1), move(right, phase, -1)), axis=1)


def small_gather(block, phase):
    far = move(block, phase, 2)
    blocks = near_gather(block, phase)
    blocks[2] = far
    return blocks


def small_sum(parts, phase):
    came = [move(parts[2], phase, 2), move(parts[1], phase, 1), move(parts[-1], phase, -1)]
    return sum([value.astype(F32) for value in came], parts[0].astype(F32))


def ring_sum(parts, near_up, near_down, phase):
    half = parts[0].shape[1] // 2
    far_up, far_down = move(parts[2][:, :half], phase, 1), move(parts[2][:, half:], phase, -1)
    up_on, down_on = lax.optimization_barrier(
        (add16(parts[1][:, :half], far_up), add16(parts[-1][:, half:], far_down))
    )
    up_on, down_on = move(up_on, phase, 1), move(down_on, phase, -1)
    left = parts[0][:, :half].astype(F32) + up_on.astype(F32) + near_down.astype(F32)
    right = parts[0][:, half:].astype(F32) + down_on.astype(F32) + near_up.astype(F32)
    return left, right


def attend_kernel(first, last, scale, shard, cached, *refs):
    if first:
        key_base, query_base, q_ref, kv_ref = refs[:4]
        rest = refs[4:]
    else:
        key_base, query_base, q_ref, kv_ref, max_in, sum_in, acc_in = refs[:7]
        rest = refs[7:]
    if last:
        out_ref, q_s, max_s, sum_s, acc_s = rest
    else:
        max_s, sum_s, acc_s, q_s = rest
    positions, width = q_ref.shape
    head = 128
    heads = width // head
    rows = positions * heads
    for h in range(heads):
        q_s[h * positions : (h + 1) * positions, :] = q_ref[:, h * head : (h + 1) * head]
    if first:
        max_s[...] = jnp.full_like(max_s, NEGATIVE)
        sum_s[...] = jnp.zeros_like(sum_s)
        acc_s[...] = jnp.zeros_like(acc_s)
    else:
        max_s[...] = max_in[...]
        sum_s[...] = sum_in[...]
        acc_s[...] = acc_in[...]
    fresh = shard - cached
    column = lax.broadcasted_iota(jnp.int32, (rows, fresh), 1)
    ahead = column - lax.broadcasted_iota(jnp.int32, (rows, fresh), 0) % positions

    @pl.loop(0, kv_ref.shape[0] // shard)
    def _(step):
        start = pl.multiple_of(step * shard, shard)
        keys = kv_ref[pl.ds(start, shard), :head]
        values = kv_ref[pl.ds(start, shard), head:]
        room = query_base[0] - key_base[step]
        raw = lax.dot_general(q_s[...], keys, NT, preferred_element_type=F32)
        late = jnp.where(ahead <= room, raw[:, cached:], NEGATIVE)
        parts = [raw[:, i * head : (i + 1) * head] for i in range(cached // head)]
        parts += [late[:, i * head : (i + 1) * head] for i in range(fresh // head)]
        old = max_s[:, :1]
        top = jnp.max(functools.reduce(jnp.maximum, parts), axis=1, keepdims=True)
        new = jnp.maximum(old, top * scale)
        shrink = jnp.exp2(old - new)
        weights = [jnp.exp2(part * scale - new) for part in parts]
        sum_s[...] = sum_s[...] * shrink + functools.reduce(jnp.add, weights)
        mixed = jnp.concatenate([part.astype(BF16) for part in weights], axis=1)
        acc_s[...] = acc_s[...] * shrink + jnp.dot(mixed, values, preferred_element_type=F32)
        max_s[...] = jnp.broadcast_to(new, max_s.shape)

    if last:
        total = jnp.sum(sum_s[...], axis=1, keepdims=True)
        mixed = (acc_s[...] / total).astype(BF16)
        for h in range(heads):
            out_ref[:, h * head : (h + 1) * head] = mixed[h * positions : (h + 1) * positions, :]


def attend(query_rows, kv_rows, key_base, query_base, state, last, shard, cached):
    positions, width = query_rows.shape
    head = 128
    rows = positions * width // head
    first = state is None
    scale = math.log2(math.e) / math.sqrt(head)
    shape = jax.ShapeDtypeStruct((rows, head), F32)
    vmem = pl.BlockSpec(memory_space=pltpu.VMEM)
    smem = pl.BlockSpec(memory_space=pltpu.SMEM)
    operands = (key_base, query_base, query_rows, kv_rows) + (() if first else tuple(state))
    keys = kv_rows.shape[0]
    scratch = [pltpu.VMEM((rows, head), BF16)]
    return pl.pallas_call(
        functools.partial(attend_kernel, first, last, scale, shard, cached),
        out_shape=jax.ShapeDtypeStruct((positions, width), BF16) if last else (shape,) * 3,
        in_specs=[smem, smem] + [vmem] * (len(operands) - 2),
        out_specs=vmem if last else (vmem,) * 3,
        scratch_shapes=scratch + ([pltpu.VMEM((rows, head), F32)] * 3 if last else []),
        compiler_params=pltpu.CompilerParams(vmem_limit_bytes=32 << 20),
        cost_estimate=pl.CostEstimate(
            flops=4 * rows * keys * head, bytes_accessed=keys * 512, transcendentals=rows * keys
        ),
    )(*operands)


def stack(blocks):
    return jnp.concatenate([blocks[d] for d in ORDER], axis=0)


def on_device(
    residual,
    queries,
    cache_kv,
    fresh_key_value,
    out_weight,
    norm_gain,
    router_weight,
    gate_weight,
    up_weight,
    down_weight,
    expert_ids,
):
    new_local = queries.shape[1]
    exp_count = lax.axis_size("exp")
    model_width = out_weight.shape[1]
    width = model_width // exp_count
    half = width // 2
    own_tokens = 2 * new_local
    ctx_index = lax.axis_index("ctx")
    z = lax.axis_index("exp")
    core = ctx_index % CORES
    lead = core == 0
    way = 1 - 2 * core
    chip_x = ctx_index // (CORES * SIDE)
    chip_y = ctx_index // CORES % SIDE

    def by_core(own, other, axis=0):
        return jnp.concatenate((jnp.where(lead, own, other), jnp.where(lead, other, own)), axis=axis)

    def mine(value):
        return jnp.where(lead, value[0], value[1])

    def theirs(value):
        return jnp.where(lead, value[1], value[0])

    cache_rows = jnp.concatenate((cache_kv[0], cache_kv[1]), axis=2)
    fresh_rows = jnp.concatenate((fresh_key_value[0], fresh_key_value[1]), axis=2)
    cached = cache_rows.shape[1]
    lanes = cache_rows.shape[2]
    q_given = theirs(queries)
    sent = jnp.concatenate(
        (theirs(cache_rows), theirs(fresh_rows), q_given[:, :lanes], q_given[:, lanes:]), axis=0
    )
    sent = swap(sent)
    came = cached + new_local
    kv_block = jnp.concatenate(
        (by_core(mine(cache_rows), sent[:cached]), by_core(mine(fresh_rows), sent[cached:came])),
        axis=0,
    )
    shard = kv_block.shape[0]
    q_came = jnp.concatenate((sent[came : came + new_local], sent[came + new_local :]), axis=1)
    query_rows = by_core(mine(queries), q_came)
    positions = query_rows.shape[0]
    query_base = ((chip_x * SIDE + chip_y) * positions).reshape(1).astype(jnp.int32)

    def key_base(distances):
        chips = []
        for far in distances:
            for near in ORDER:
                dx, dy = jnp.where(lead, near, far), jnp.where(lead, far, near)
                chips.append(ctx_id(chip_x + dx + SIDE, chip_y + dy + SIDE, 0) // CORES)
        return (jnp.stack(chips) * positions).astype(jnp.int32)

    gate_own, up_own, down_own = gate_weight[0].T, up_weight[0].T, down_weight[0]
    residual_own = residual.reshape(own_tokens, width)
    picked_own = jnp.transpose(expert_ids, (1, 0, 2)).reshape(own_tokens, 2)

    line = small_gather(kv_block, 0)
    line, gate_sent, up_sent, down_sent = lax.optimization_barrier(
        (line, gate_own, up_own, down_own)
    )
    gate_other, up_other, down_other = swap(gate_sent), swap(up_sent), swap(down_sent)
    rows_near = stack(line)
    blocks = near_gather(rows_near, 1)
    state = attend(query_rows, rows_near, key_base((0,)), query_base, None, False, shard, 2 * cached)
    blocks[-1], blocks[1], state = lax.optimization_barrier((blocks[-1], blocks[1], state))
    far = far_gather(blocks, 1)
    rows_mid = jnp.concatenate((blocks[-1], blocks[1]), axis=0)
    state = attend(query_rows, rows_mid, key_base((-1, 1)), query_base, state, False, shard, 2 * cached)
    query_rows, gate_other, up_other, down_other = lax.optimization_barrier(
        (query_rows, gate_other, up_other, down_other)
    )
    attended = attend(query_rows, far, key_base((2,)), query_base, state, True, shard, 2 * cached)

    ours, others = attended[:new_local], attended[new_local:]
    ours, others = jnp.where(lead, ours, others), jnp.where(lead, others, ours)
    heads = by_core(ours, swap(others))

    capacity = own_tokens * 2 // exp_count
    experts = jnp.arange(exp_count, dtype=jnp.int32)
    named = jnp.any(picked_own[:, :, None] == experts, axis=1)
    order = jnp.cumsum(named.astype(jnp.int32), axis=0) - 1
    slots = jnp.arange(capacity, dtype=jnp.int32)
    chosen = named.T[:, None, :] & (order.T[:, None, :] == slots[None, :, None])
    selector = chosen.reshape(exp_count * capacity, own_tokens).astype(BF16)

    chosen_heads = jnp.dot(selector, heads, preferred_element_type=F32).astype(BF16)
    chosen_residual = jnp.dot(selector, residual_own, preferred_element_type=F32)
    product = jnp.dot(chosen_heads, out_weight, preferred_element_type=F32).astype(BF16)
    here = lax.dynamic_slice_in_dim(out_weight, z * width, width, 1)
    here = jnp.dot(chosen_heads, here, preferred_element_type=F32) + chosen_residual
    product = lax.dynamic_update_slice_in_dim(product, here.astype(BF16), z * width, 1)
    product = product.reshape(exp_count, capacity, model_width)

    def share(distance):
        index = (z + distance + exp_count) % exp_count
        return lax.dynamic_index_in_dim(product, index, 0, keepdims=False).astype(F32)

    top = exp_count // 2
    middle = model_width // 2
    def z_start(up, down):
        up, down = jnp.where(lead, up, down), jnp.where(lead, down, up)
        up, down = lax.optimization_barrier((up.astype(BF16), down.astype(BF16)))
        return z_move(up, 1), z_move(down, -1)

    def z_end(came):
        one, two = came[0].astype(F32), came[1].astype(F32)
        return jnp.where(lead, one, two), jnp.where(lead, two, one)

    opposite = share(top)
    up, down = z_end(z_start(opposite[:, :middle], opposite[:, middle:]))
    up_share, down_share = share(top - 1), share(1 - top)
    up = jnp.concatenate((up_share[:, :middle] + up, up_share[:, middle:]), axis=1)
    down = jnp.concatenate((down_share[:, :middle], down_share[:, middle:] + down), axis=1)
    gate_other = lax.optimization_barrier((gate_other, product))[0]
    waiting = [(gate_own, gate_other), (up_own, up_other), (down_own, down_other)]
    pairs = []
    for distance in range(top - 1, 0, -1):
        pair = jnp.concatenate(waiting[len(pairs)], axis=0)
        came, pair = lax.optimization_barrier((z_start(up, down), pair))
        pairs.append(pair)
        if len(pairs) < len(waiting):
            own, other = waiting[len(pairs)]
            waiting[len(pairs)] = (own, lax.optimization_barrier((other, came))[0])
        up, down = z_end(came)
        if distance > 1:
            up, down = up + share(distance - 1), down + share(1 - distance)
    gate_both, up_both, down_both = pairs
    rows = share(0) + up + down
    normed = (
        rows * lax.rsqrt(jnp.mean(rows * rows, axis=1, keepdims=True) + EPSILON) * norm_gain
    ).astype(BF16)

    logits = jnp.dot(normed, router_weight, preferred_element_type=F32)
    own_slots = lax.dynamic_index_in_dim(chosen, z, 0, keepdims=False)
    other_id = jnp.sum(picked_own, axis=1) - z
    other_of_row = jnp.sum(jnp.where(own_slots, other_id[None, :], 0), axis=1)
    own_logit = jnp.sum(jnp.where(experts[None, :] == z, logits, 0.0), axis=1)
    other_logit = jnp.sum(jnp.where(experts[None, :] == other_of_row[:, None], logits, 0.0), axis=1)
    gate_values = jax.nn.sigmoid(own_logit - other_logit)
    first = jnp.any(own_slots & (picked_own[:, 0] == z)[None, :], axis=1)

    def activate(block):
        gate = lax.dot_general(block, gate_both, NT, preferred_element_type=F32)
        active = lax.dot_general(block, up_both, NT, preferred_element_type=F32)
        gate, active = lax.optimization_barrier((gate, active))
        return (jax.nn.silu(gate) * active).astype(BF16)

    def project(active):
        return jnp.dot(active, down_both, preferred_element_type=F32).astype(BF16)

    token_line = stack(small_gather(normed, 0))
    count = token_line.shape[0]
    blocks = near_gather(token_line, 1)
    parts = {0: project(activate(token_line))}
    blocks[-1], blocks[1], parts[0] = lax.optimization_barrier((blocks[-1], blocks[1], parts[0]))
    far = far_gather(blocks, 1)
    near = project(activate(jnp.concatenate((blocks[-1], blocks[1]), axis=0)))
    near = lax.optimization_barrier(near)
    far = lax.optimization_barrier((far, near))[0]
    parts[-1], parts[1] = near[:count], near[count:]
    near_up, near_down = move(parts[1][:, middle:], 1, 1), move(parts[-1][:, :middle], 1, -1)
    active, near_up, near_down = lax.optimization_barrier((activate(far), near_up, near_down))
    parts[2] = lax.optimization_barrier(project(active))
    line = [value.astype(BF16) for value in ring_sum(parts, near_up, near_down, 1)]
    line = jnp.concatenate(lax.optimization_barrier(line), axis=1)
    line = lax.optimization_barrier(line)
    returned = small_sum(
        {d: line[i * capacity : (i + 1) * capacity] for i, d in enumerate(ORDER)}, 0
    )
    returned = returned.astype(BF16).astype(F32)

    scaled = gate_values[:, None] * returned + jnp.where(first[:, None], rows, 0.0)
    scaled = scaled.astype(BF16)

    def pick(distance, start=0, size=width):
        column = (z + distance + exp_count) % exp_count * width + start
        return lax.dynamic_slice_in_dim(scaled, column, size, 1)

    for_other = [pick(-way * distance) for distance in range(1, top)]
    for_other = jnp.concatenate(for_other + [pick(top, (1 - core) * half, half)], axis=1)
    for_this = [pick(way * distance) for distance in range(1, top)]
    for_this = jnp.concatenate(for_this + [pick(top, core * half, half)], axis=1)
    both = by_core(for_this, swap(for_other))
    came = [
        z_move(both[:, (distance - 1) * width : distance * width], distance)
        for distance in range(1, top + 1)
    ]
    came = jnp.concatenate(came, axis=1)
    keep = jnp.where(lead, came[:capacity], came[capacity:])
    give = swap(jnp.where(lead, came[capacity:], came[:capacity]))
    low, high = jnp.where(lead, keep, give), jnp.where(lead, give, keep)
    cut = [slice(i * width, (i + 1) * width) for i in range(top - 1)]
    rest = slice((top - 1) * width, None)
    across = jnp.concatenate((low[:, rest], high[:, rest]), axis=1)
    around = [pick(0)] + [high[:, c] for c in cut] + [across] + [low[:, c] for c in cut][::-1]
    home = jnp.roll(jnp.stack(around, axis=0), z, axis=0).reshape(exp_count * capacity, width)
    result = lax.dot_general(selector, home, (((0,), (0,)), ((), ())), preferred_element_type=F32)
    return result.astype(BF16).reshape(2, new_local, width)


def solution(mesh):
    placed = (
        P(None, "ctx", "exp"),
        P(None, "ctx", "exp"),
        P(None, None, "ctx", "exp"),
        P(None, None, "ctx", "exp"),
        P("exp", None),
        P(),
        P(),
        P("exp", None, "ctx"),
        P("exp", None, "ctx"),
        P("exp", "ctx", None),
        P("ctx", None, None),
    )
    return jax.shard_map(
        on_device, mesh=mesh, in_specs=placed, out_specs=P(None, "ctx", "exp"), check_vma=False
    )
```

```python
import functools
import math

import jax
import jax.numpy as jnp
from jax import lax
from jax.experimental import pallas as pl
from jax.experimental.pallas import tpu as pltpu
from jax.sharding import PartitionSpec as P

EPSILON = 1e-05
NEGATIVE = -1e30
SIDE = 4
CORES = 2
BF16 = jnp.bfloat16
F32 = jnp.float32
NT = (((1,), (1,)), ((), ()))


def ctx_id(x, y, core):
    return ((x % SIDE) * SIDE + y % SIDE) * CORES + core


def ring_pairs(phase, step):
    pairs = []
    for x in range(SIDE):
        for y in range(SIDE):
            for core in range(CORES):
                dx, dy = (step, 0) if phase == core else (0, step)
                pairs.append((ctx_id(x, y, core), ctx_id(x + dx, y + dy, core)))
    return pairs


SWAP = [(i, i ^ 1) for i in range(SIDE * SIDE * CORES)]
ORDER = (0, -1, 1, 2)


def move(value, phase, step):
    return lax.ppermute(value, "ctx", ring_pairs(phase, step))


def swap(value):
    return lax.ppermute(value, "ctx", SWAP)


def z_move(value, step):
    count = lax.axis_size("exp")
    pairs = []
    for device in range(SIDE * SIDE * CORES):
        way = step if device % CORES == 0 else -step
        pairs += [(device * count + z, device * count + (z + way) % count) for z in range(count)]
    return lax.ppermute(value, ("ctx", "exp"), pairs)


def add16(a, b):
    return (a.astype(F32) + b.astype(F32)).astype(BF16)


def near_gather(block, phase):
    return {0: block, -1: move(block, phase, 1), 1: move(block, phase, -1)}


def far_gather(blocks, phase):
    half = blocks[0].shape[1] // 2
    left, right = blocks[-1][:, :half], blocks[1][:, half:]
    return jnp.concatenate((move(left, phase, 1), move(right, phase, -1)), axis=1)


def small_gather(block, phase):
    far = move(block, phase, 2)
    blocks = near_gather(block, phase)
    blocks[2] = far
    return blocks


def small_sum(parts, phase):
    came = [move(parts[2], phase, 2), move(parts[1], phase, 1), move(parts[-1], phase, -1)]
    return sum([value.astype(F32) for value in came], parts[0].astype(F32))


def ring_sum(parts, near_up, near_down, phase):
    half = parts[0].shape[1] // 2
    far_up, far_down = move(parts[2][0], phase, 1), move(parts[2][1], phase, -1)
    up_on, down_on = lax.optimization_barrier(
        (add16(parts[1][:, :half], far_up), add16(parts[-1][:, half:], far_down))
    )
    up_on, down_on = move(up_on, phase, 1), move(down_on, phase, -1)
    left = parts[0][:, :half].astype(F32) + up_on.astype(F32) + near_down.astype(F32)
    right = parts[0][:, half:].astype(F32) + down_on.astype(F32) + near_up.astype(F32)
    return left, right


def attend_kernel(first, last, scale, shard, cached, *refs):
    if first:
        key_base, query_base, q_ref, kv_ref = refs[:4]
        rest = refs[4:]
    else:
        key_base, query_base, q_ref, kv_ref, max_in, sum_in, acc_in = refs[:7]
        rest = refs[7:]
    if last:
        out_ref, q_s, max_s, sum_s, acc_s = rest
    else:
        max_s, sum_s, acc_s, q_s = rest
    positions, width = q_ref.shape
    head = 128
    heads = width // head
    rows = positions * heads
    for h in range(heads):
        q_s[h * positions : (h + 1) * positions, :] = q_ref[:, h * head : (h + 1) * head]
    if first:
        max_s[...] = jnp.full_like(max_s, NEGATIVE)
        sum_s[...] = jnp.zeros_like(sum_s)
        acc_s[...] = jnp.zeros_like(acc_s)
    else:
        max_s[...] = max_in[...]
        sum_s[...] = sum_in[...]
        acc_s[...] = acc_in[...]
    fresh = shard - cached
    column = lax.broadcasted_iota(jnp.int32, (rows, fresh), 1)
    ahead = column - lax.broadcasted_iota(jnp.int32, (rows, fresh), 0) % positions

    @pl.loop(0, kv_ref.shape[0] // shard)
    def _(step):
        start = pl.multiple_of(step * shard, shard)
        keys = kv_ref[pl.ds(start, shard), :head]
        values = kv_ref[pl.ds(start, shard), head:]
        room = query_base[0] - key_base[step]
        raw = lax.dot_general(q_s[...], keys, NT, preferred_element_type=F32)
        late = jnp.where(ahead <= room, raw[:, cached:], NEGATIVE)
        parts = [raw[:, i * head : (i + 1) * head] for i in range(cached // head)]
        parts += [late[:, i * head : (i + 1) * head] for i in range(fresh // head)]
        old = max_s[:, :1]
        top = jnp.max(functools.reduce(jnp.maximum, parts), axis=1, keepdims=True)
        new = jnp.maximum(old, top * scale)
        shrink = jnp.exp2(old - new)
        weights = [jnp.exp2(part * scale - new) for part in parts]
        sum_s[...] = sum_s[...] * shrink + functools.reduce(jnp.add, weights)
        mixed = jnp.concatenate([part.astype(BF16) for part in weights], axis=1)
        acc_s[...] = acc_s[...] * shrink + jnp.dot(mixed, values, preferred_element_type=F32)
        max_s[...] = jnp.broadcast_to(new, max_s.shape)

    if last:
        total = jnp.sum(sum_s[...], axis=1, keepdims=True)
        mixed = (acc_s[...] / total).astype(BF16)
        for h in range(heads):
            out_ref[:, h * head : (h + 1) * head] = mixed[h * positions : (h + 1) * positions, :]


def attend(query_rows, kv_rows, key_base, query_base, state, last, shard, cached):
    positions, width = query_rows.shape
    head = 128
    rows = positions * width // head
    first = state is None
    scale = math.log2(math.e) / math.sqrt(head)
    shape = jax.ShapeDtypeStruct((rows, head), F32)
    vmem = pl.BlockSpec(memory_space=pltpu.VMEM)
    smem = pl.BlockSpec(memory_space=pltpu.SMEM)
    operands = (key_base, query_base, query_rows, kv_rows) + (() if first else tuple(state))
    keys = kv_rows.shape[0]
    scratch = [pltpu.VMEM((rows, head), BF16)]
    return pl.pallas_call(
        functools.partial(attend_kernel, first, last, scale, shard, cached),
        out_shape=jax.ShapeDtypeStruct((positions, width), BF16) if last else (shape,) * 3,
        in_specs=[smem, smem] + [vmem] * (len(operands) - 2),
        out_specs=vmem if last else (vmem,) * 3,
        scratch_shapes=scratch + ([pltpu.VMEM((rows, head), F32)] * 3 if last else []),
        compiler_params=pltpu.CompilerParams(vmem_limit_bytes=32 << 20),
        cost_estimate=pl.CostEstimate(
            flops=4 * rows * keys * head, bytes_accessed=keys * 512, transcendentals=rows * keys
        ),
    )(*operands)


def stack(blocks):
    return jnp.concatenate([blocks[d] for d in ORDER], axis=0)


def on_device(
    residual,
    queries,
    cache_kv,
    fresh_key_value,
    out_weight,
    norm_gain,
    router_weight,
    gate_weight,
    up_weight,
    down_weight,
    expert_ids,
):
    new_local = queries.shape[1]
    exp_count = lax.axis_size("exp")
    model_width = out_weight.shape[1]
    width = model_width // exp_count
    half = width // 2
    own_tokens = 2 * new_local
    ctx_index = lax.axis_index("ctx")
    z = lax.axis_index("exp")
    core = ctx_index % CORES
    lead = core == 0
    way = 1 - 2 * core
    chip_x = ctx_index // (CORES * SIDE)
    chip_y = ctx_index // CORES % SIDE

    def by_core(own, other, axis=0):
        return jnp.concatenate((jnp.where(lead, own, other), jnp.where(lead, other, own)), axis=axis)

    def mine(value):
        return jnp.where(lead, value[0], value[1])

    def theirs(value):
        return jnp.where(lead, value[1], value[0])

    cache_rows = jnp.concatenate((cache_kv[0], cache_kv[1]), axis=2)
    fresh_rows = jnp.concatenate((fresh_key_value[0], fresh_key_value[1]), axis=2)
    cached = cache_rows.shape[1]
    lanes = cache_rows.shape[2]
    q_given = theirs(queries)
    sent = jnp.concatenate(
        (theirs(cache_rows), theirs(fresh_rows), q_given[:, :lanes], q_given[:, lanes:]), axis=0
    )
    sent = swap(sent)
    came = cached + new_local
    kv_block = jnp.concatenate(
        (by_core(mine(cache_rows), sent[:cached]), by_core(mine(fresh_rows), sent[cached:came])),
        axis=0,
    )
    shard = kv_block.shape[0]
    q_came = jnp.concatenate((sent[came : came + new_local], sent[came + new_local :]), axis=1)
    query_rows = by_core(mine(queries), q_came)
    positions = query_rows.shape[0]
    query_base = ((chip_x * SIDE + chip_y) * positions).reshape(1).astype(jnp.int32)

    def key_base(distances):
        chips = []
        for far in distances:
            for near in ORDER:
                dx, dy = jnp.where(lead, near, far), jnp.where(lead, far, near)
                chips.append(ctx_id(chip_x + dx + SIDE, chip_y + dy + SIDE, 0) // CORES)
        return (jnp.stack(chips) * positions).astype(jnp.int32)

    gate_own, up_own, down_own = gate_weight[0].T, up_weight[0].T, down_weight[0]
    residual_own = residual.reshape(own_tokens, width)
    picked_own = jnp.transpose(expert_ids, (1, 0, 2)).reshape(own_tokens, 2)

    line = small_gather(kv_block, 0)
    rows_near = stack(line)
    blocks = near_gather(rows_near, 1)
    state = attend(query_rows, rows_near, key_base((0,)), query_base, None, False, shard, 2 * cached)
    blocks[-1], blocks[1], state, *given = lax.optimization_barrier(
        (blocks[-1], blocks[1], state, gate_own, up_own, down_own)
    )
    far = far_gather(blocks, 1)
    gate_other, up_other, down_other = [swap(value) for value in given]
    rows_mid = jnp.concatenate((blocks[-1], blocks[1]), axis=0)
    state = attend(query_rows, rows_mid, key_base((-1, 1)), query_base, state, False, shard, 2 * cached)
    attended = attend(query_rows, far, key_base((2,)), query_base, state, True, shard, 2 * cached)

    ours, others = attended[:new_local], attended[new_local:]
    ours, others = jnp.where(lead, ours, others), jnp.where(lead, others, ours)
    heads = by_core(ours, swap(others))

    capacity = own_tokens * 2 // exp_count
    experts = jnp.arange(exp_count, dtype=jnp.int32)
    named = jnp.any(picked_own[:, :, None] == experts, axis=1)
    order = jnp.cumsum(named.astype(jnp.int32), axis=0) - 1
    slots = jnp.arange(capacity, dtype=jnp.int32)
    chosen = named.T[:, None, :] & (order.T[:, None, :] == slots[None, :, None])
    selector = chosen.reshape(exp_count * capacity, own_tokens).astype(BF16)

    chosen_heads = jnp.dot(selector, heads, preferred_element_type=F32).astype(BF16)
    chosen_residual = jnp.dot(selector, residual_own, preferred_element_type=F32)
    top = exp_count // 2
    middle = model_width // 2

    def with_residual(rows, own_columns):
        columns = lax.dynamic_slice_in_dim(rows, z * width, width, 1).astype(F32) + own_columns
        return lax.dynamic_update_slice_in_dim(rows, columns.astype(rows.dtype), z * width, 1)

    start = (z + top) % exp_count * capacity
    opposite = jnp.dot(
        lax.dynamic_slice_in_dim(chosen_heads, start, capacity, 0),
        out_weight,
        preferred_element_type=F32,
    )
    opposite = with_residual(
        opposite, lax.dynamic_slice_in_dim(chosen_residual, start, capacity, 0)
    )
    chosen_heads, opposite = lax.optimization_barrier((chosen_heads, opposite))
    product = jnp.dot(chosen_heads, out_weight, preferred_element_type=F32).astype(BF16)
    product = with_residual(product, chosen_residual)
    product = product.reshape(exp_count, capacity, model_width)

    def share(distance):
        index = (z + distance + exp_count) % exp_count
        return lax.dynamic_index_in_dim(product, index, 0, keepdims=False).astype(F32)

    def z_start(up, down):
        up, down = jnp.where(lead, up, down), jnp.where(lead, down, up)
        up, down = lax.optimization_barrier((up.astype(BF16), down.astype(BF16)))
        return z_move(up, 1), z_move(down, -1)

    def z_end(came):
        one, two = came[0].astype(F32), came[1].astype(F32)
        return jnp.where(lead, one, two), jnp.where(lead, two, one)

    up, down = z_end(z_start(opposite[:, :middle], opposite[:, middle:]))
    up_share, down_share = share(top - 1), share(1 - top)
    up = jnp.concatenate((up_share[:, :middle] + up, up_share[:, middle:]), axis=1)
    down = jnp.concatenate((down_share[:, :middle], down_share[:, middle:] + down), axis=1)
    gate_other, up_other, down_other, product = lax.optimization_barrier(
        (gate_other, up_other, down_other, product)
    )
    waiting = [(gate_own, gate_other), (up_own, up_other), (down_own, down_other)]
    pairs = []
    for distance in range(top - 1, 0, -1):
        pair = jnp.concatenate(waiting[len(pairs)], axis=0)
        came, pair = lax.optimization_barrier((z_start(up, down), pair))
        pairs.append(pair)
        if len(pairs) < len(waiting):
            own, other = waiting[len(pairs)]
            waiting[len(pairs)] = (own, lax.optimization_barrier((other, came))[0])
        up, down = z_end(came)
        if distance > 1:
            up, down = up + share(distance - 1), down + share(1 - distance)
    gate_both, up_both, down_both = pairs
    rows = share(0) + up + down
    normed = (
        rows * lax.rsqrt(jnp.mean(rows * rows, axis=1, keepdims=True) + EPSILON) * norm_gain
    ).astype(BF16)

    logits = jnp.dot(normed, router_weight, preferred_element_type=F32)
    own_slots = lax.dynamic_index_in_dim(chosen, z, 0, keepdims=False)
    other_id = jnp.sum(picked_own, axis=1) - z
    other_of_row = jnp.sum(jnp.where(own_slots, other_id[None, :], 0), axis=1)
    own_logit = jnp.sum(jnp.where(experts[None, :] == z, logits, 0.0), axis=1)
    other_logit = jnp.sum(jnp.where(experts[None, :] == other_of_row[:, None], logits, 0.0), axis=1)
    gate_values = jax.nn.sigmoid(own_logit - other_logit)
    first = jnp.any(own_slots & (picked_own[:, 0] == z)[None, :], axis=1)

    def activate(block):
        gate = lax.dot_general(block, gate_both, NT, preferred_element_type=F32)
        active = lax.dot_general(block, up_both, NT, preferred_element_type=F32)
        gate, active = lax.optimization_barrier((gate, active))
        return (jax.nn.silu(gate) * active).astype(BF16)

    def project(active):
        return jnp.dot(active, down_both, preferred_element_type=F32).astype(BF16)

    token_line = stack(small_gather(normed, 0))
    count = token_line.shape[0]
    blocks = near_gather(token_line, 1)
    parts = {0: project(activate(token_line))}
    blocks[-1], blocks[1], parts[0] = lax.optimization_barrier((blocks[-1], blocks[1], parts[0]))
    far = far_gather(blocks, 1)
    near = project(activate(jnp.concatenate((blocks[-1], blocks[1]), axis=0)))
    near = lax.optimization_barrier(near)
    far = lax.optimization_barrier((far, near))[0]
    parts[-1], parts[1] = near[:count], near[count:]
    near_up, near_down = move(parts[1][:, middle:], 1, 1), move(parts[-1][:, :middle], 1, -1)
    active, near_up, near_down = lax.optimization_barrier((activate(far), near_up, near_down))
    parts[2] = lax.optimization_barrier(
        [
            jnp.dot(active, down, preferred_element_type=F32).astype(BF16)
            for down in (down_both[:, :middle], down_both[:, middle:])
        ]
    )
    line = [value.astype(BF16) for value in ring_sum(parts, near_up, near_down, 1)]
    line = jnp.concatenate(lax.optimization_barrier(line), axis=1)
    line = lax.optimization_barrier(line)
    returned = small_sum(
        {d: line[i * capacity : (i + 1) * capacity] for i, d in enumerate(ORDER)}, 0
    )
    returned = returned.astype(BF16).astype(F32)

    scaled = gate_values[:, None] * returned + jnp.where(first[:, None], rows, 0.0)
    scaled = scaled.astype(BF16)

    def pick(distance, start=0, size=width):
        column = (z + distance + exp_count) % exp_count * width + start
        return lax.dynamic_slice_in_dim(scaled, column, size, 1)

    for_other = [pick(-way * distance) for distance in range(1, top)]
    for_other = jnp.concatenate(for_other + [pick(top, (1 - core) * half, half)], axis=1)
    for_this = [pick(way * distance) for distance in range(1, top)]
    for_this = jnp.concatenate(for_this + [pick(top, core * half, half)], axis=1)
    both = by_core(for_this, swap(for_other))
    came = [
        z_move(both[:, (distance - 1) * width : distance * width], distance)
        for distance in range(1, top + 1)
    ]
    came = jnp.concatenate(came, axis=1)
    keep = jnp.where(lead, came[:capacity], came[capacity:])
    give = swap(jnp.where(lead, came[capacity:], came[:capacity]))
    low, high = jnp.where(lead, keep, give), jnp.where(lead, give, keep)
    cut = [slice(i * width, (i + 1) * width) for i in range(top - 1)]
    rest = slice((top - 1) * width, None)
    across = jnp.concatenate((low[:, rest], high[:, rest]), axis=1)
    around = [pick(0)] + [high[:, c] for c in cut] + [across] + [low[:, c] for c in cut][::-1]
    home = jnp.roll(jnp.stack(around, axis=0), z, axis=0).reshape(exp_count * capacity, width)
    result = lax.dot_general(selector, home, (((0,), (0,)), ((), ())), preferred_element_type=F32)
    return result.astype(BF16).reshape(2, new_local, width)


def solution(mesh):
    placed = (
        P(None, "ctx", "exp"),
        P(None, "ctx", "exp"),
        P(None, None, "ctx", "exp"),
        P(None, None, "ctx", "exp"),
        P("exp", None),
        P(),
        P(),
        P("exp", None, "ctx"),
        P("exp", None, "ctx"),
        P("exp", "ctx", None),
        P("ctx", None, None),
    )
    return jax.shard_map(
        on_device, mesh=mesh, in_specs=placed, out_specs=P(None, "ctx", "exp"), check_vma=False
    )
```

```python
import functools
import math

import jax
import jax.numpy as jnp
from jax import lax
from jax.experimental import pallas as pl
from jax.experimental.pallas import tpu as pltpu
from jax.sharding import PartitionSpec as P

EPSILON = 1e-05
NEGATIVE = -1e30
SIDE = 4
CORES = 2
BF16 = jnp.bfloat16
F32 = jnp.float32
NT = (((1,), (1,)), ((), ()))


def ctx_id(x, y, core):
    return ((x % SIDE) * SIDE + y % SIDE) * CORES + core


def ring_pairs(phase, step):
    pairs = []
    for x in range(SIDE):
        for y in range(SIDE):
            for core in range(CORES):
                dx, dy = (step, 0) if phase == core else (0, step)
                pairs.append((ctx_id(x, y, core), ctx_id(x + dx, y + dy, core)))
    return pairs


SWAP = [(i, i ^ 1) for i in range(SIDE * SIDE * CORES)]
ORDER = (0, -1, 1, 2)


def move(value, phase, step):
    return lax.ppermute(value, "ctx", ring_pairs(phase, step))


def swap(value):
    return lax.ppermute(value, "ctx", SWAP)


def z_move(value, step):
    count = lax.axis_size("exp")
    pairs = []
    for device in range(SIDE * SIDE * CORES):
        way = step if device % CORES == 0 else -step
        pairs += [(device * count + z, device * count + (z + way) % count) for z in range(count)]
    return lax.ppermute(value, ("ctx", "exp"), pairs)


def add16(a, b):
    return (a.astype(F32) + b.astype(F32)).astype(BF16)


def near_gather(block, phase):
    return {0: block, -1: move(block, phase, 1), 1: move(block, phase, -1)}


def far_gather(blocks, phase):
    half = blocks[0].shape[1] // 2
    left, right = blocks[-1][:, :half], blocks[1][:, half:]
    return jnp.concatenate((move(left, phase, 1), move(right, phase, -1)), axis=1)


def small_gather(block, phase):
    far = move(block, phase, 2)
    blocks = near_gather(block, phase)
    blocks[2] = far
    return blocks


def small_sum(parts, phase):
    came = [move(parts[2], phase, 2), move(parts[1], phase, 1), move(parts[-1], phase, -1)]
    return sum([value.astype(F32) for value in came], parts[0].astype(F32))


def attend_kernel(first, last, scale, shard, cached, *refs):
    if first:
        key_base, query_base, q_ref, kv_ref = refs[:4]
        rest = refs[4:]
    else:
        key_base, query_base, q_ref, kv_ref, max_in, sum_in, acc_in = refs[:7]
        rest = refs[7:]
    if last:
        out_ref, q_s, max_s, sum_s, acc_s = rest
    else:
        max_s, sum_s, acc_s, q_s = rest
    positions, width = q_ref.shape
    head = 128
    heads = width // head
    rows = positions * heads
    for h in range(heads):
        q_s[h * positions : (h + 1) * positions, :] = q_ref[:, h * head : (h + 1) * head]
    if first:
        max_s[...] = jnp.full_like(max_s, NEGATIVE)
        sum_s[...] = jnp.zeros_like(sum_s)
        acc_s[...] = jnp.zeros_like(acc_s)
    else:
        max_s[...] = max_in[...]
        sum_s[...] = sum_in[...]
        acc_s[...] = acc_in[...]
    fresh = shard - cached
    column = lax.broadcasted_iota(jnp.int32, (rows, fresh), 1)
    ahead = column - lax.broadcasted_iota(jnp.int32, (rows, fresh), 0) % positions

    @pl.loop(0, kv_ref.shape[0] // shard)
    def _(step):
        start = pl.multiple_of(step * shard, shard)
        keys = kv_ref[pl.ds(start, shard), :head]
        values = kv_ref[pl.ds(start, shard), head:]
        room = query_base[0] - key_base[step]
        raw = lax.dot_general(q_s[...], keys, NT, preferred_element_type=F32)
        late = jnp.where(ahead <= room, raw[:, cached:], NEGATIVE)
        parts = [raw[:, i * head : (i + 1) * head] for i in range(cached // head)]
        parts += [late[:, i * head : (i + 1) * head] for i in range(fresh // head)]
        old = max_s[:, :1]
        top = jnp.max(functools.reduce(jnp.maximum, parts), axis=1, keepdims=True)
        new = jnp.maximum(old, top * scale)
        shrink = jnp.exp2(old - new)
        weights = [jnp.exp2(part * scale - new) for part in parts]
        sum_s[...] = sum_s[...] * shrink + functools.reduce(jnp.add, weights)
        mixed = jnp.concatenate([part.astype(BF16) for part in weights], axis=1)
        acc_s[...] = acc_s[...] * shrink + jnp.dot(mixed, values, preferred_element_type=F32)
        max_s[...] = jnp.broadcast_to(new, max_s.shape)

    if last:
        total = jnp.sum(sum_s[...], axis=1, keepdims=True)
        mixed = (acc_s[...] / total).astype(BF16)
        for h in range(heads):
            out_ref[:, h * head : (h + 1) * head] = mixed[h * positions : (h + 1) * positions, :]


def attend(query_rows, kv_rows, key_base, query_base, state, last, shard, cached):
    positions, width = query_rows.shape
    head = 128
    rows = positions * width // head
    first = state is None
    scale = math.log2(math.e) / math.sqrt(head)
    shape = jax.ShapeDtypeStruct((rows, head), F32)
    vmem = pl.BlockSpec(memory_space=pltpu.VMEM)
    smem = pl.BlockSpec(memory_space=pltpu.SMEM)
    operands = (key_base, query_base, query_rows, kv_rows) + (() if first else tuple(state))
    keys = kv_rows.shape[0]
    scratch = [pltpu.VMEM((rows, head), BF16)]
    return pl.pallas_call(
        functools.partial(attend_kernel, first, last, scale, shard, cached),
        out_shape=jax.ShapeDtypeStruct((positions, width), BF16) if last else (shape,) * 3,
        in_specs=[smem, smem] + [vmem] * (len(operands) - 2),
        out_specs=vmem if last else (vmem,) * 3,
        scratch_shapes=scratch + ([pltpu.VMEM((rows, head), F32)] * 3 if last else []),
        compiler_params=pltpu.CompilerParams(vmem_limit_bytes=32 << 20),
        cost_estimate=pl.CostEstimate(
            flops=4 * rows * keys * head, bytes_accessed=keys * 512, transcendentals=rows * keys
        ),
    )(*operands)


def stack(blocks):
    return jnp.concatenate([blocks[d] for d in ORDER], axis=0)


def on_device(
    residual,
    queries,
    cache_kv,
    fresh_key_value,
    out_weight,
    norm_gain,
    router_weight,
    gate_weight,
    up_weight,
    down_weight,
    expert_ids,
):
    new_local = queries.shape[1]
    exp_count = lax.axis_size("exp")
    model_width = out_weight.shape[1]
    width = model_width // exp_count
    half = width // 2
    own_tokens = 2 * new_local
    ctx_index = lax.axis_index("ctx")
    z = lax.axis_index("exp")
    core = ctx_index % CORES
    lead = core == 0
    way = 1 - 2 * core
    chip_x = ctx_index // (CORES * SIDE)
    chip_y = ctx_index // CORES % SIDE

    def by_core(own, other, axis=0):
        return jnp.concatenate((jnp.where(lead, own, other), jnp.where(lead, other, own)), axis=axis)

    def mine(value):
        return jnp.where(lead, value[0], value[1])

    def theirs(value):
        return jnp.where(lead, value[1], value[0])

    cache_rows = jnp.concatenate((cache_kv[0], cache_kv[1]), axis=2)
    fresh_rows = jnp.concatenate((fresh_key_value[0], fresh_key_value[1]), axis=2)
    cached = cache_rows.shape[1]
    lanes = cache_rows.shape[2]
    q_given = theirs(queries)
    sent = jnp.concatenate(
        (theirs(cache_rows), theirs(fresh_rows), q_given[:, :lanes], q_given[:, lanes:]), axis=0
    )
    sent = swap(sent)
    came = cached + new_local
    kv_block = jnp.concatenate(
        (by_core(mine(cache_rows), sent[:cached]), by_core(mine(fresh_rows), sent[cached:came])),
        axis=0,
    )
    shard = kv_block.shape[0]
    q_came = jnp.concatenate((sent[came : came + new_local], sent[came + new_local :]), axis=1)
    query_rows = by_core(mine(queries), q_came)
    positions = query_rows.shape[0]
    query_base = ((chip_x * SIDE + chip_y) * positions).reshape(1).astype(jnp.int32)

    def key_base(distances):
        chips = []
        for far in distances:
            for near in ORDER:
                dx, dy = jnp.where(lead, near, far), jnp.where(lead, far, near)
                chips.append(ctx_id(chip_x + dx + SIDE, chip_y + dy + SIDE, 0) // CORES)
        return (jnp.stack(chips) * positions).astype(jnp.int32)

    gate_own, up_own, down_own = gate_weight[0].T, up_weight[0].T, down_weight[0]
    residual_own = residual.reshape(own_tokens, width)
    picked_own = jnp.transpose(expert_ids, (1, 0, 2)).reshape(own_tokens, 2)

    line = small_gather(kv_block, 0)
    rows_near = stack(line)
    blocks = near_gather(rows_near, 1)
    state = attend(query_rows, rows_near, key_base((0,)), query_base, None, False, shard, 2 * cached)
    blocks[-1], blocks[1], state, *given = lax.optimization_barrier(
        (blocks[-1], blocks[1], state, gate_own, up_own, down_own)
    )
    far = far_gather(blocks, 1)
    gate_other, up_other, down_other = [swap(value) for value in given]
    rows_mid = jnp.concatenate((blocks[-1], blocks[1]), axis=0)
    state = attend(query_rows, rows_mid, key_base((-1, 1)), query_base, state, False, shard, 2 * cached)
    attended = attend(query_rows, far, key_base((2,)), query_base, state, True, shard, 2 * cached)

    ours, others = attended[:new_local], attended[new_local:]
    ours, others = jnp.where(lead, ours, others), jnp.where(lead, others, ours)
    heads = by_core(ours, swap(others))

    capacity = own_tokens * 2 // exp_count
    experts = jnp.arange(exp_count, dtype=jnp.int32)
    named = jnp.any(picked_own[:, :, None] == experts, axis=1)
    order = jnp.cumsum(named.astype(jnp.int32), axis=0) - 1
    slots = jnp.arange(capacity, dtype=jnp.int32)
    chosen = named.T[:, None, :] & (order.T[:, None, :] == slots[None, :, None])
    selector = chosen.reshape(exp_count * capacity, own_tokens).astype(BF16)

    chosen_heads = jnp.dot(selector, heads, preferred_element_type=F32).astype(BF16)
    chosen_residual = jnp.dot(selector, residual_own, preferred_element_type=F32)
    top = exp_count // 2
    middle = model_width // 2

    def with_residual(rows, own_columns):
        columns = lax.dynamic_slice_in_dim(rows, z * width, width, 1).astype(F32) + own_columns
        return lax.dynamic_update_slice_in_dim(rows, columns.astype(rows.dtype), z * width, 1)

    start = (z + top) % exp_count * capacity
    opposite = jnp.dot(
        lax.dynamic_slice_in_dim(chosen_heads, start, capacity, 0),
        out_weight,
        preferred_element_type=F32,
    )
    opposite = with_residual(
        opposite, lax.dynamic_slice_in_dim(chosen_residual, start, capacity, 0)
    )
    chosen_heads, opposite = lax.optimization_barrier((chosen_heads, opposite))
    product = jnp.dot(chosen_heads, out_weight, preferred_element_type=F32).astype(BF16)
    product = with_residual(product, chosen_residual)
    product = product.reshape(exp_count, capacity, model_width)

    def share(distance):
        index = (z + distance + exp_count) % exp_count
        return lax.dynamic_index_in_dim(product, index, 0, keepdims=False).astype(F32)

    def z_start(up, down):
        up, down = jnp.where(lead, up, down), jnp.where(lead, down, up)
        up, down = lax.optimization_barrier((up.astype(BF16), down.astype(BF16)))
        return z_move(up, 1), z_move(down, -1)

    def z_end(came):
        one, two = came[0].astype(F32), came[1].astype(F32)
        return jnp.where(lead, one, two), jnp.where(lead, two, one)

    up, down = z_end(z_start(opposite[:, :middle], opposite[:, middle:]))
    up_share, down_share = share(top - 1), share(1 - top)
    up = jnp.concatenate((up_share[:, :middle] + up, up_share[:, middle:]), axis=1)
    down = jnp.concatenate((down_share[:, :middle], down_share[:, middle:] + down), axis=1)
    gate_other, up_other, down_other, product = lax.optimization_barrier(
        (gate_other, up_other, down_other, product)
    )
    waiting = [(gate_own, gate_other), (up_own, up_other), (down_own, down_other)]
    pairs = []
    for distance in range(top - 1, 0, -1):
        pair = jnp.concatenate(waiting[len(pairs)], axis=0)
        came, pair = lax.optimization_barrier((z_start(up, down), pair))
        pairs.append(pair)
        if len(pairs) < len(waiting):
            own, other = waiting[len(pairs)]
            waiting[len(pairs)] = (own, lax.optimization_barrier((other, came))[0])
        up, down = z_end(came)
        if distance > 1:
            up, down = up + share(distance - 1), down + share(1 - distance)
    gate_both, up_both, down_both = pairs
    rows = share(0) + up + down
    normed = (
        rows * lax.rsqrt(jnp.mean(rows * rows, axis=1, keepdims=True) + EPSILON) * norm_gain
    ).astype(BF16)

    logits = jnp.dot(normed, router_weight, preferred_element_type=F32)
    own_slots = lax.dynamic_index_in_dim(chosen, z, 0, keepdims=False)
    other_id = jnp.sum(picked_own, axis=1) - z
    other_of_row = jnp.sum(jnp.where(own_slots, other_id[None, :], 0), axis=1)
    own_logit = jnp.sum(jnp.where(experts[None, :] == z, logits, 0.0), axis=1)
    other_logit = jnp.sum(jnp.where(experts[None, :] == other_of_row[:, None], logits, 0.0), axis=1)
    gate_values = jax.nn.sigmoid(own_logit - other_logit)
    first = jnp.any(own_slots & (picked_own[:, 0] == z)[None, :], axis=1)

    def activate(block):
        gate = lax.dot_general(block, gate_both, NT, preferred_element_type=F32)
        active = lax.dot_general(block, up_both, NT, preferred_element_type=F32)
        gate, active = lax.optimization_barrier((gate, active))
        return (jax.nn.silu(gate) * active).astype(BF16)

    def project(active):
        return jnp.dot(active, down_both, preferred_element_type=F32).astype(BF16)

    token_line = stack(small_gather(normed, 0))
    count = token_line.shape[0]
    blocks = near_gather(token_line, 1)
    parts = {0: project(activate(token_line))}
    blocks[-1], blocks[1], parts[0] = lax.optimization_barrier((blocks[-1], blocks[1], parts[0]))
    cuts = [slice(0, count // 2), slice(count // 2, count)]
    far = [far_gather({d: blocks[d][cuts[0]] for d in (0, -1, 1)}, 1)]
    active = activate(jnp.concatenate((blocks[-1], blocks[1]), axis=0))
    later = {d: blocks[d][cuts[1]] for d in (0, -1, 1)}
    near, later = lax.optimization_barrier((project(active), later))
    far.append(far_gather(later, 1))
    parts[-1], parts[1] = near[:count], near[count:]
    near_up, near_down = move(parts[1][:, middle:], 1, 1), move(parts[-1][:, :middle], 1, -1)

    def far_product(block, *others):
        active = activate(lax.optimization_barrier((block,) + others)[0])
        return [
            jnp.dot(active, down, preferred_element_type=F32).astype(BF16)
            for down in (down_both[:, :middle], down_both[:, middle:])
        ]

    def further(cut, far_up, far_down):
        up, down = lax.optimization_barrier(
            (add16(parts[1][cut, :middle], far_up), add16(parts[-1][cut, middle:], far_down))
        )
        return move(up, 1, 1), move(down, 1, -1)

    one = lax.optimization_barrier(far_product(far[0], near))
    gone = move(one[0], 1, 1), move(one[1], 1, -1)
    gone, two = lax.optimization_barrier((gone, far_product(far[1], one[0], one[1])))
    sums = [further(cuts[0], *gone)]
    gone = move(two[0], 1, 1), move(two[1], 1, -1)
    gone, sums[0], near_up, near_down = lax.optimization_barrier(
        (gone, sums[0], near_up, near_down)
    )
    sums.append(further(cuts[1], *gone))
    back = []
    for cut, (up, down) in zip(cuts, sums):
        left = parts[0][cut, :middle].astype(F32) + up.astype(F32) + near_down[cut].astype(F32)
        right = parts[0][cut, middle:].astype(F32) + down.astype(F32) + near_up[cut].astype(F32)
        halves = lax.optimization_barrier((left.astype(BF16), right.astype(BF16)))
        whole = lax.optimization_barrier(jnp.concatenate(halves, axis=1))
        back += [whole[:capacity], whole[capacity:]]
    returned = small_sum(dict(zip(ORDER, back)), 0)
    returned = returned.astype(BF16).astype(F32)

    scaled = gate_values[:, None] * returned + jnp.where(first[:, None], rows, 0.0)
    scaled = scaled.astype(BF16)

    def pick(distance, start=0, size=width):
        column = (z + distance + exp_count) % exp_count * width + start
        return lax.dynamic_slice_in_dim(scaled, column, size, 1)

    for_other = [pick(-way * distance) for distance in range(1, top)]
    for_other = jnp.concatenate(for_other + [pick(top, (1 - core) * half, half)], axis=1)
    for_this = [pick(way * distance) for distance in range(1, top)]
    for_this = jnp.concatenate(for_this + [pick(top, core * half, half)], axis=1)
    both = by_core(for_this, swap(for_other))
    came = [
        z_move(both[:, (distance - 1) * width : distance * width], distance)
        for distance in range(1, top + 1)
    ]
    came = jnp.concatenate(came, axis=1)
    keep = jnp.where(lead, came[:capacity], came[capacity:])
    give = swap(jnp.where(lead, came[capacity:], came[:capacity]))
    low, high = jnp.where(lead, keep, give), jnp.where(lead, give, keep)
    cut = [slice(i * width, (i + 1) * width) for i in range(top - 1)]
    rest = slice((top - 1) * width, None)
    across = jnp.concatenate((low[:, rest], high[:, rest]), axis=1)
    around = [pick(0)] + [high[:, c] for c in cut] + [across] + [low[:, c] for c in cut][::-1]
    home = jnp.roll(jnp.stack(around, axis=0), z, axis=0).reshape(exp_count * capacity, width)
    result = lax.dot_general(selector, home, (((0,), (0,)), ((), ())), preferred_element_type=F32)
    return result.astype(BF16).reshape(2, new_local, width)


def solution(mesh):
    placed = (
        P(None, "ctx", "exp"),
        P(None, "ctx", "exp"),
        P(None, None, "ctx", "exp"),
        P(None, None, "ctx", "exp"),
        P("exp", None),
        P(),
        P(),
        P("exp", None, "ctx"),
        P("exp", None, "ctx"),
        P("exp", "ctx", None),
        P("ctx", None, None),
    )
    return jax.shard_map(
        on_device, mesh=mesh, in_specs=placed, out_specs=P(None, "ctx", "exp"), check_vma=False
    )
```
